512 devices in a mesh: grp: 16 (over x, z_lo), ep: 32 (over z_hi, y, core).
Axes of the slice: x: 4, y: 4, z: 16 (z_hi: 4, z_lo: 4; z = z_hi * 4 + z_lo), core: 2. Of those that a mesh axis runs over, the one named last changes fastest.
Arguments:
- tokens: bfloat16 [8192, 2048], P('ep'), may hold values from -6 to 6
- routes: int32 [8192, 8], P('ep'), may hold values from 0 to 63, all different within a row; in each aligned block of 256 rows (0 to 255, 256 to 511, ...) at most 48 rows name the same one
- gate_values: float32 [8192, 8], P('ep'), may hold values from 0.05 to 0.3
- old_group: int32 [64], replicated, may hold values from 0 to 15, as said below
- move_mask: int32 [4], replicated, may hold values from 0 to 15
- pair_index: int32 [8192], replicated, may hold values from 0 to 8191, each once
- reward_head: bfloat16 [2048], replicated, may hold values from -0.125 to 0.125
- w_up: bfloat16 [16, 2048, 4096], P('grp', None, 'ep'), may hold values from -0.125 to 0.125
- w_down: bfloat16 [16, 4096, 2048], P('grp', 'ep'), may hold values from -0.1875 to 0.1875
- acc_up: bfloat16 [16, 2048, 4096], P('grp', None, 'ep'), may hold values from -6 to 6
- acc_down: bfloat16 [16, 4096, 2048], P('grp', 'ep'), may hold values from -6 to 6
Outputs:
- new_acc_up: bfloat16 [16, 2048, 4096], P('grp', None, 'ep')
- new_acc_down: bfloat16 [16, 4096, 2048], P('grp', 'ep')
- pair_loss: float32 [], replicated
The draws below stay inside these ranges and needn't reach their ends.
Inputs may be any that keep to these rules, and one draw needn't show every extreme that they name: `routes`: in the rows of one device (aligned blocks of 256 rows), no expert is named by more than 48 rows, a bound that some block reaches. `old_group`: for each l, the experts e with e % 4 == l lie in 16 different groups. `pair_index`: every token appears once.
All inputs are finite; a program needn't handle non-finite values.
Results may differ from the reference program's by a relative error of at most 0.0048.
Values may be sent and summed in bfloat16 or wider, within the bound.
No kernel may reach another device: no remote copies, remote signals or barrier semaphores. Data moves between devices by JAX's collectives and lax.ppermute only.
A program may use at most 64 MiB of HBM per device.

```python
import math
import jax
import jax.numpy as jnp
import numpy as np
from jax import lax

D = 2048
HID_DEV = 128
EXP_GRP = 4
TOP = 8
TOK_DEV = 256
HID = 1024
EXPERTS = 64
TOKENS = 8192
PAIRS = 4096
CAP = 48
N_GRP = 16
N_EP = 32


def draw_old_group(key, part):
    key = jax.random.fold_in(key, 11)
    subkeys = jax.random.split(key, EXP_GRP)
    orders = jax.vmap(jax.random.permutation, in_axes=(0, None))(subkeys, N_GRP)
    return orders.T.reshape(-1).astype(jnp.int32)


def draw_move_mask(key, part):
    key = jax.random.fold_in(key, 23)
    draw_key, pick_key = jax.random.split(key)
    values = jax.random.randint(draw_key, (EXP_GRP,), 0, N_GRP)
    chosen_slot = jax.random.randint(pick_key, (), 0, EXP_GRP)
    return jnp.where(jnp.arange(EXP_GRP) == chosen_slot, N_GRP - 1, values).astype(jnp.int32)


def steps_of(key, extent, cuts, low, largest):
    def one(dim, parts):
        heights = jax.random.uniform(jax.random.fold_in(jax.random.fold_in(key, 6), dim), (parts,), jnp.float32, low / len(cuts), largest / len(cuts))
        return jnp.repeat(jnp.exp(heights), extent[dim] // parts).reshape((-1,) + (1,) * (len(extent) - dim - 1))

    factor_of = one(*cuts[0])
    for cut in cuts[1:]:
        factor_of = factor_of * one(*cut)
    return factor_of


def shared_out(key, own, number, rows, amount, top, bound, lean):
    sequence = jax.random.permutation(key, amount)
    heavy_load, usual = portions_of(amount, rows * top, bound, lean, True), portions_of(amount, rows * top, bound, lean, False)
    places = jnp.arange(amount)

    def named(lengths, rotation):
        used = int((lengths > 0).sum())
        fixed = max(1, used // 4)
        passed = fixed + (places - fixed + rotation * (used - fixed)) % max(1, amount - fixed)
        return jnp.zeros((amount,), jnp.int32).at[sequence[jnp.where(places < fixed, places, passed)]].set(jnp.asarray(lengths, jnp.int32))

    lengths = jnp.where(number % 4 == 0, named(heavy_load, number // 4), named(usual, number - number // 4 - 1))
    mixed = jax.random.permutation(jax.random.fold_in(own, 3), amount)
    source_of, sink = mixed[0:amount // 2 * 2:2], mixed[1:amount // 2 * 2:2]
    room = jnp.minimum(lengths[source_of] - 1, bound - lengths[sink]) // 2
    room = jnp.where((source_of == sequence[0]) | (sink == sequence[0]) | (lengths[sink] == 0), 0, jnp.maximum(room, 0))
    passed = jax.random.randint(jax.random.fold_in(own, 4), (amount // 2,), 0, 1 << 20) % (room + 1)
    lengths = lengths.at[source_of].add(-passed).at[sink].add(passed)
    items = jnp.searchsorted(jnp.cumsum(lengths), jnp.arange(rows * top), side="right").astype(jnp.int32)
    listing = items.reshape(top, rows).T
    listing = listing[jax.random.permutation(jax.random.fold_in(own, 1), rows)]
    rotation = jax.random.randint(jax.random.fold_in(own, 2), (rows, 1), 0, top)
    return jnp.take_along_axis(listing, (jnp.arange(top)[None, :] + rotation) % top, axis=1)


def portions_of(number_of, total, most, slope, full):
    portions = [(1 << 20) // math.isqrt(grade ** slope) + 1 for grade in range(1, number_of + 1)]
    largest = most if full else min(most, max(-(-total // number_of), total * portions[0] // sum(portions)))
    least = 1 if total - largest >= number_of - 1 else 0
    given, spare = [largest] + [least] * (number_of - 1), total - largest - least * (number_of - 1)
    while spare > 0:
        candidates = [i for i in range(1, number_of) if given[i] < largest] or [i for i in range(1, number_of) if given[i] < most]
        whole, remaining = sum([portions[i] for i in candidates]), spare
        for i in candidates:
            addition = min(most - given[i], max(1, remaining * portions[i] // whole), spare)
            given[i] = given[i] + addition
            spare = spare - addition
    return np.array(given)


def bell_draw(own_key, shape, deviation, limit, cuts=(), held_as=jnp.bfloat16):
    result = deviation * jax.random.normal(own_key, shape, jnp.float32)
    if cuts:
        result = result * steps_of(own_key, shape, cuts, -0.22, 0.18)
    return jnp.clip(result, -limit, limit).astype(held_as)


def setup_inputs(seed: int = 0) -> dict:
    splits = jax.random.split(jax.random.key(seed), 12)
    tokens = bell_draw(splits[0], (TOKENS, D), 1.0, 6.0, ((0, 32),))
    routes_keys = jax.random.split(jax.random.fold_in(splits[1], 1), TOKENS // TOK_DEV)
    routes_turns = jax.random.permutation(jax.random.fold_in(splits[1], 3), TOKENS // TOK_DEV)
    routes = jax.vmap(lambda own, number: shared_out(jax.random.fold_in(splits[1], 2), own, number, TOK_DEV, EXPERTS, TOP, CAP, 2))(routes_keys, routes_turns).reshape((TOKENS, TOP))
    gate_values = jnp.clip(0.05 + 0.25 * jax.random.uniform(splits[2], (TOKENS, TOP), jnp.float32) ** steps_of(splits[2], (TOKENS, TOP), ((0, 32),), -0.2, 0.2), 0.05, 0.3)
    old_group = draw_old_group(jax.random.fold_in(splits[11], 71), 0)
    move_mask = draw_move_mask(jax.random.fold_in(splits[11], 71), 0)
    pair_index = jax.random.permutation(splits[5], TOKENS).astype(jnp.int32)
    reward_head = bell_draw(splits[6], (D,), D ** -0.5, 0.125)
    w_up = bell_draw(splits[7], (N_GRP, D, EXP_GRP * HID), D ** -0.5, 0.125, ((0, 16), (2, 32)))
    w_down = bell_draw(splits[8], (N_GRP, EXP_GRP * HID, D), HID ** -0.5, 0.1875, ((0, 16), (1, 32)))
    acc_up = bell_draw(splits[9], (N_GRP, D, EXP_GRP * HID), 1.0, 6.0, ((0, 16), (2, 32)))
    acc_down = bell_draw(splits[10], (N_GRP, EXP_GRP * HID, D), 1.0, 6.0, ((0, 16), (1, 32)))
    return dict(tokens=tokens, routes=routes, gate_values=gate_values, old_group=old_group, move_mask=move_mask, pair_index=pair_index, reward_head=reward_head, w_up=w_up, w_down=w_down, acc_up=acc_up, acc_down=acc_down)


loss_scale = 64.0
highest = lax.Precision.HIGHEST


def silu_slope(pre_act):
    sigmoid_value = jax.nn.sigmoid(pre_act)
    return sigmoid_value * (1.0 + pre_act * (1.0 - sigmoid_value))


def reference(tokens, routes, gate_values, old_group, move_mask, pair_index, reward_head, w_up, w_down, acc_up, acc_down):
    hidden_width = N_EP // EXP_GRP * HID_DEV
    row_limit = N_EP * CAP
    up_slots = w_up.reshape(N_GRP, D, EXP_GRP, hidden_width)
    down_slots = w_down.reshape(N_GRP, EXP_GRP, hidden_width, D)
    up_accum = acc_up.reshape(N_GRP, D, EXP_GRP, hidden_width)
    down_accum = acc_down.reshape(N_GRP, EXP_GRP, hidden_width, D)
    expert_ids = jnp.arange(EXPERTS, dtype=jnp.int32)
    local_slot = expert_ids % EXP_GRP

    def gather_rows(expert_id):
        row_hits = routes == expert_id
        row_found = jnp.any(row_hits, axis=1)
        row_ids = jnp.nonzero(row_found, size=row_limit, fill_value=0)[0].astype(jnp.int32)
        row_valid = jnp.arange(row_limit) < jnp.sum(row_found.astype(jnp.int32))
        gate_row = jnp.sum(jnp.where(row_hits, gate_values, jnp.float32(0.0)), axis=1)[row_ids]
        return row_ids, gate_row * row_valid.astype(jnp.float32)

    def expert_core(expert_id):
        row_ids, gate_row = gather_rows(expert_id)
        owner_group = old_group[expert_id]
        slot_index = local_slot[expert_id]
        rows_in = tokens[row_ids]
        up_block = up_slots[owner_group, :, slot_index, :]
        pre_act = jnp.dot(rows_in, up_block, preferred_element_type=jnp.float32)
        hidden = jax.nn.silu(pre_act).astype(jnp.bfloat16)
        head_proj = jnp.dot(down_slots[owner_group, slot_index], reward_head, preferred_element_type=jnp.float32)
        return row_ids, gate_row, rows_in, pre_act, hidden, head_proj, owner_group, slot_index

    def expert_forward(expert_id):
        row_ids, gate_row, rows_in, pre_act, hidden, head_proj, owner_group, slot_index = expert_core(expert_id)
        partial_value = jnp.dot(hidden.astype(jnp.float32), head_proj, precision=highest)
        return row_ids, gate_row * partial_value

    row_table, reward_terms = lax.map(expert_forward, expert_ids)
    base_reward = jnp.dot(tokens, reward_head, preferred_element_type=jnp.float32)
    routed = jnp.zeros((TOKENS,), jnp.float32).at[row_table.reshape(-1)].add(reward_terms.reshape(-1))
    rewards = base_reward + routed
    chosen = pair_index[:PAIRS]
    rejected = pair_index[PAIRS:]
    margin = rewards[chosen] - rewards[rejected]
    pair_loss = jnp.mean(jax.nn.softplus(-margin))
    weight_grad = loss_scale * jax.nn.sigmoid(-margin)
    token_grad = jnp.zeros((TOKENS,), jnp.float32).at[chosen].set(-weight_grad).at[rejected].set(weight_grad)

    def expert_backward(expert_id):
        row_ids, gate_row, rows_in, pre_act, hidden, head_proj, owner_group, slot_index = expert_core(expert_id)
        grad_in = token_grad[row_ids] * gate_row
        hidden_grad = jnp.dot(grad_in, hidden.astype(jnp.float32), precision=highest)
        grad_down = hidden_grad[:, None] * reward_head.astype(jnp.float32)[None, :]
        new_down = (down_accum[owner_group, slot_index].astype(jnp.float32) + grad_down).astype(jnp.bfloat16)
        pre_grad = (grad_in[:, None] * head_proj[None, :] * silu_slope(pre_act)).astype(jnp.bfloat16)
        grad_up = lax.dot_general(rows_in, pre_grad, (((0,), (0,)), ((), ())), preferred_element_type=jnp.float32)
        new_up = (up_accum[owner_group, :, slot_index, :].astype(jnp.float32) + grad_up).astype(jnp.bfloat16)
        return new_up, new_down

    new_up, new_down = lax.map(expert_backward, expert_ids)
    new_group = jnp.bitwise_xor(old_group, move_mask[local_slot])
    slot_owner = jnp.zeros((N_GRP, EXP_GRP), jnp.int32).at[new_group, local_slot].set(expert_ids)
    out_up = new_up[slot_owner].transpose(0, 2, 1, 3).reshape(N_GRP, D, EXP_GRP * hidden_width)
    out_down = new_down[slot_owner].reshape(N_GRP, EXP_GRP * hidden_width, D)
    return out_up, out_down, pair_loss
```

```python
import jax
import jax.numpy as jnp
from jax import lax
from jax.experimental import pallas as pl
from jax.experimental.pallas import tpu as pltpu
from jax.sharding import Mesh
from jax.sharding import PartitionSpec as P

D = 2048
HID_DEV = 128
EXP_GRP = 4
TOK_DEV = 256
CAP = 48
WIDE = D + 128
ROWS = 16 * CAP
PAIRS = 4096

f32 = jnp.float32
bf16 = jnp.bfloat16
VMEM = pl.BlockSpec(memory_space=pltpu.VMEM)
SMEM = pl.BlockSpec(memory_space=pltpu.SMEM)
PARAMS = pltpu.CompilerParams(vmem_limit_bytes=48 * 1024 * 1024)
NT = (((1,), (1,)), ((), ()))

BLOCKS = (
    [(CAP * d, 0, d) for d in range(4)]
    + [(4 * CAP + 2 * CAP * d + CAP * i, k, d) for d in range(4) for i, k in enumerate((1, 3))]
    + [(12 * CAP + CAP * d, 2, d) for d in range(4)]
)


def shape(dims, kind):
    return jax.ShapeDtypeStruct(dims, kind)


def iota(dims, axis):
    return lax.broadcasted_iota(jnp.int32, dims, axis)


def thirds(value):
    first = value.astype(bf16).astype(f32)
    second = (value - first).astype(bf16).astype(f32)
    third = (value - first - second).astype(bf16).astype(f32)
    return first, second, third


def weights_kernel(up_ref, down_ref, head_ref, out_ref):
    out_ref[:D, :] = up_ref[...]
    head = jnp.broadcast_to(head_ref[...], (16, D))
    proj = lax.dot_general(head, down_ref[...], NT, preferred_element_type=f32)
    first, second, third = thirds(proj)
    row = iota((16, HID_DEV), 0)
    packed = jnp.where(row == 0, first, jnp.where(row == 1, second, jnp.where(row == 2, third, 0.0)))
    out_ref[D:, :] = packed.astype(bf16)


def dispatch_kernel(group_ref, mask_ref, info_ref, tok_ref, routes_ref, gates_ref, pair_ref, head_ref, *outs):
    out_refs, base_ref = outs[:4], outs[4]
    grp, zh, member = info_ref[0], info_ref[1], info_ref[2]
    routes = routes_ref[...]
    gates = gates_ref[...]
    sel, gate = [], []
    for k in range(EXP_GRP):
        slot = zh ^ k
        mask = mask_ref[slot]
        expert = jnp.int32(0)
        for j in range(16):
            found = (group_ref[4 * j + slot] ^ mask) == grp
            expert = jnp.where(found, 4 * j + slot, expert)
        hit = routes == expert
        sel.append(jnp.sum(jnp.where(hit, 1.0, 0.0), axis=0, keepdims=True))
        gate.append(jnp.sum(jnp.where(hit, gates, 0.0), axis=0, keepdims=True))
    row8 = iota((8, TOK_DEV), 0)
    chosen = jnp.zeros((8, TOK_DEV), f32)
    for k in range(EXP_GRP):
        chosen = jnp.where(row8 == k, sel[k], chosen)
    tri = jnp.where(iota((TOK_DEV, TOK_DEV), 0) <= iota((TOK_DEV, TOK_DEV), 1), 1.0, 0.0).astype(bf16)
    place = jnp.dot(chosen.astype(bf16), tri, preferred_element_type=f32) - 1.0
    own = (iota((TOK_DEV, 1), 0) + member * TOK_DEV).astype(f32)

    def look(r, code):
        first = pair_ref[pl.ds(r, 1), :]
        second = pair_ref[pl.ds(r + 32, 1), :]
        return jnp.where(first == own, second + 1.0, jnp.where(second == own, -1.0 - first, code))

    code = lax.fori_loop(0, 32, look, jnp.zeros((TOK_DEV, 128), f32), unroll=4)
    code = jnp.sum(code, axis=1, keepdims=True)
    partner = jnp.abs(code) - 1.0
    high = jnp.floor(partner * (1.0 / TOK_DEV))
    low = partner - high * TOK_DEV
    lane = iota((TOK_DEV, 128), 1)
    by_token = jnp.where(lane == 13, high, jnp.where(lane == 14, low, jnp.where(lane == 15, jnp.where(code > 0, 1.0, -1.0), 0.0)))
    by_token = jnp.where(lane == 0, iota((TOK_DEV, 128), 0).astype(f32), by_token).astype(bf16)
    rows = iota((128, TOK_DEV), 0)
    by_slot = jnp.zeros((128, TOK_DEV), f32)
    for k in range(EXP_GRP):
        for j, part in enumerate(thirds(gate[k])):
            by_slot = jnp.where(rows == 1 + 3 * k + j, part, by_slot)
    by_slot = by_slot.astype(bf16)
    base_ref[...] = lax.dot_general(
        jnp.broadcast_to(head_ref[...], (16, D)), tok_ref[...], NT, preferred_element_type=f32
    )[:8]
    height = iota((CAP, TOK_DEV), 0).astype(f32)
    picks = [
        jnp.where((place[k : k + 1] == height) & (sel[k] > 0.5), 1.0, 0.0).astype(bf16) for k in range(EXP_GRP)
    ]
    pick = jnp.concatenate(picks, axis=0)
    notes = jnp.dot(pick, by_token, preferred_element_type=f32) + lax.dot_general(
        pick, by_slot, NT, preferred_element_type=f32
    )
    wide = jnp.dot(pick, tok_ref[...], preferred_element_type=f32)
    for k in range(EXP_GRP):
        out_refs[k][:, :D] = wide[CAP * k : CAP * (k + 1)].astype(bf16)
        out_refs[k][:, D:] = notes[CAP * k : CAP * (k + 1)].astype(bf16)


def forward_kernel(info_ref, base_ref, own_w_ref, other_w_ref, *refs):
    groups, (x_ref, slope_ref, hid_ref, note_ref, part_ref, u_ref) = refs[:12], refs[12:]
    grp, zh, y = info_ref[0], info_ref[1], info_ref[3]
    u_ref[:, :HID_DEV] = own_w_ref[:D, :]
    u_ref[:, HID_DEV:] = other_w_ref[:D, :]
    start = 0
    for ref in groups:
        count = ref.shape[0]
        x_ref[start : start + count, :] = ref[:, :D]
        note_ref[start : start + count, :] = ref[:, D:].astype(f32)
        start += count
    pieces = jnp.concatenate([own_w_ref[D:, :], other_w_ref[D:, :]], axis=1).astype(f32)
    proj = pieces[0:1] + pieces[1:2] + pieces[2:3]
    pre = jnp.dot(x_ref[...], u_ref[...], preferred_element_type=f32)
    sig = jax.nn.sigmoid(pre)
    hidden = (pre * sig).astype(bf16)
    hid_ref[...] = hidden
    slope_ref[...] = proj * (sig * (1.0 + pre * (1.0 - sig)))
    value = jnp.sum(hidden.astype(f32) * proj, axis=1, keepdims=True)
    lane = iota((CAP, 128), 1)
    token = iota((CAP, TOK_DEV), 1).astype(f32)
    row = iota((16, TOK_DEV), 0)
    total = jnp.where((row == zh * 4 + y) & (grp == 0), base_ref[0:1, :], 0.0)
    for at, k, d in BLOCKS:
        note = note_ref[at : at + CAP, :]
        gate = jnp.sum(jnp.where((lane >= 1 + 3 * k) & (lane < 4 + 3 * k), note, 0.0), axis=1, keepdims=True)
        term = gate * value[at : at + CAP]
        spread = jnp.sum(jnp.where(note[:, 0:1] == token, term, 0.0), axis=0, keepdims=True)
        total = total + jnp.where(row == (zh ^ k) * 4 + (y ^ d), spread, 0.0)
    part_ref[...] = total


def backward_kernel(info_ref, table_ref, x_ref, slope_ref, hid_ref, note_ref, own_ref, send_ref, own_head_ref):
    zh, c, y = info_ref[1], info_ref[4], info_ref[3]
    table = table_ref[...]
    note = note_ref[...]
    token = iota((CAP, TOK_DEV), 1).astype(f32)
    lane = iota((CAP, 128), 1)
    mine, gates = [], []
    for at, k, d in BLOCKS:
        block = ((zh ^ k) * 4 + (y ^ d)) * 2 + c
        values = table_ref[pl.ds(block, 1), :]
        part = note_ref[at : at + CAP, :]
        mine.append(jnp.sum(jnp.where(part[:, 0:1] == token, values, 0.0), axis=1, keepdims=True))
        gates.append(
            jnp.sum(jnp.where((lane >= 1 + 3 * k) & (lane < 4 + 3 * k), part, 0.0), axis=1, keepdims=True)
        )
    mine = jnp.concatenate(mine, axis=0)
    gate = jnp.concatenate(gates, axis=0)
    hot = jnp.where(iota((ROWS, 32), 1).astype(f32) == note[:, 13:14], 1.0, 0.0).astype(bf16)
    found = jnp.zeros((ROWS, TOK_DEV), f32)
    for part in thirds(table):
        found = found + jnp.dot(hot, part.astype(bf16), preferred_element_type=f32)
    places = iota((ROWS, TOK_DEV), 1).astype(f32)
    theirs = jnp.sum(jnp.where(places == note[:, 14:15], found, 0.0), axis=1, keepdims=True)
    side = note[:, 15:16]
    margin = side * (mine - theirs)
    grad = -side * (64.0 * jax.nn.sigmoid(-margin)) * gate
    hid_grad = jnp.sum(grad * hid_ref[...].astype(f32), axis=0, keepdims=True)
    pre_grad = (grad * slope_ref[...]).astype(bf16)
    out = lax.dot_general(x_ref[...], pre_grad, (((0,), (0,)), ((), ())), preferred_element_type=f32)
    own_ref[...] = out[:, :HID_DEV]
    send_ref[:D, :] = out[:, HID_DEV:]
    own_head_ref[...] = jnp.broadcast_to(hid_grad[:, :HID_DEV], (8, HID_DEV))
    send_ref[D:, :] = jnp.broadcast_to(hid_grad[:, HID_DEV:], (8, HID_DEV))


def loss_kernel(table_ref, pair_ref, out_ref):
    parts = jnp.concatenate([p.astype(bf16) for p in thirds(table_ref[...])], axis=0)

    def rewards_of(index):
        high = jnp.floor(index * (1.0 / TOK_DEV))
        low = index - high * TOK_DEV
        count = index.shape[1]
        row = iota((96, count), 0) & 31
        hot = jnp.where(row.astype(f32) == high, 1.0, 0.0).astype(bf16)
        found = lax.dot_general(parts, hot, (((0,), (0,)), ((), ())), preferred_element_type=f32)
        return jnp.sum(jnp.where(iota((TOK_DEV, count), 0).astype(f32) == low, found, 0.0), axis=0, keepdims=True)

    def step(r, total):
        margin = rewards_of(pair_ref[pl.ds(r, 1), :]) - rewards_of(pair_ref[pl.ds(r + 8, 1), :])
        return total + jnp.maximum(-margin, 0.0) + jnp.log1p(jnp.exp(-jnp.abs(margin)))

    total = lax.fori_loop(0, 8, step, jnp.zeros((1, 512), f32))
    out_ref[...] = jnp.broadcast_to(jnp.sum(total, axis=1, keepdims=True) * (1.0 / PAIRS), (1, 128))


def final_kernel(up_ref, down_ref, own_ref, recv_ref, own_head_ref, head_ref, new_up_ref, new_down_ref):
    new_up_ref[...] = (up_ref[...].astype(f32) + (own_ref[...] + recv_ref[:D, :])).astype(bf16)
    grad = own_head_ref[0:1] + recv_ref[D : D + 1, :]
    square = (HID_DEV, HID_DEV)
    column = jnp.sum(jnp.where(iota(square, 0) == iota(square, 1), grad, 0.0), axis=1, keepdims=True)
    new_down_ref[...] = (down_ref[...].astype(f32) + column * head_ref[...].astype(f32)).astype(bf16)


def swap(block, axis, mask):
    count = lax.axis_size(axis)
    return lax.ppermute(block, axis, [(i, i ^ mask) for i in range(count)])


def relocate(block, stages):
    for axis, mask, take in stages:
        block = jnp.where(take, swap(block, axis, mask), block)
    return block


def body(tokens, routes, gate_values, old_group, move_mask, pair_index, reward_head, w_up, w_down, acc_up, acc_down):
    x, zl, zh, y, c = (lax.axis_index(a) for a in ("x", "zl", "zh", "y", "c"))
    info = jnp.stack([x * 4 + zl, zh, zh * 8 + y * 2 + c, y, c]).astype(jnp.int32)
    head = reward_head.reshape(1, D)
    mask = jnp.sum(jnp.where(jnp.arange(EXP_GRP) == zh, move_mask, 0))
    bit = [jnp.bitwise_and(jnp.right_shift(mask, i), 1) for i in range(4)]
    by_x = [("x", 1, jnp.bitwise_xor(bit[2], bit[3]) == 1), ("x", 3, bit[3] == 1)]
    by_z = [("zl", 1, bit[0] == 1), ("zl", 2, bit[1] == 1)]

    weights = pl.pallas_call(
        weights_kernel,
        out_shape=shape((D + 16, HID_DEV), bf16),
        in_specs=[VMEM] * 3,
        out_specs=VMEM,
        compiler_params=PARAMS,
        name="weights",
    )(w_up[0], w_down[0], head)
    weights = relocate(weights, by_x + by_z)
    other_weights = swap(weights, "c", 1)

    pairs = pair_index.astype(f32)
    *sent, base = pl.pallas_call(
        dispatch_kernel,
        out_shape=[shape((CAP, WIDE), bf16)] * 4 + [shape((8, TOK_DEV), f32)],
        in_specs=[SMEM] * 3 + [VMEM] * 5,
        out_specs=[VMEM] * 5,
        compiler_params=PARAMS,
        name="dispatch",
    )(old_group, move_mask, info, tokens, routes.T, gate_values.T, pairs.reshape(64, 128), head)
    far = swap(sent[2], "zh", 2)
    near = jnp.concatenate([swap(sent[1], "zh", 1), swap(sent[3], "zh", 3)], axis=0)
    held = []
    for group in (sent[0], near, far):
        held += [group] + [swap(group, "y", d) for d in (1, 2, 3)]

    xs, slope, hidden, notes, part = pl.pallas_call(
        forward_kernel,
        out_shape=[
            shape((ROWS, D), bf16),
            shape((ROWS, 2 * HID_DEV), f32),
            shape((ROWS, 2 * HID_DEV), bf16),
            shape((ROWS, 128), f32),
            shape((16, TOK_DEV), f32),
        ],
        in_specs=[SMEM] + [VMEM] * 15,
        out_specs=[VMEM] * 5,
        scratch_shapes=[pltpu.VMEM((D, 2 * HID_DEV), bf16)],
        compiler_params=PARAMS,
        name="forward",
    )(info, base, weights, other_weights, *held)

    mine = lax.all_to_all(part, ("x", "y"), 0, 0, tiled=True)
    mine = jnp.broadcast_to(jnp.sum(mine, axis=0, keepdims=True), (16, TOK_DEV))
    mine = lax.all_to_all(mine, ("zl", "zh"), 0, 0, tiled=True)
    mine = jnp.broadcast_to(jnp.sum(mine, axis=0, keepdims=True), (32, TOK_DEV))
    table = lax.all_to_all(mine, ("x", "y", "c"), 0, 0, tiled=True)

    own, send, own_head = pl.pallas_call(
        backward_kernel,
        out_shape=[shape((D, HID_DEV), f32), shape((D + 8, HID_DEV), f32), shape((8, HID_DEV), f32)],
        in_specs=[SMEM] + [VMEM] * 5,
        out_specs=[VMEM] * 3,
        compiler_params=PARAMS,
        name="backward",
    )(info, table, xs, slope, hidden, notes)
    recv = swap(send, "c", 1)
    loss = pl.pallas_call(
        loss_kernel,
        out_shape=shape((1, 128), f32),
        in_specs=[VMEM] * 2,
        out_specs=VMEM,
        compiler_params=PARAMS,
        name="loss",
    )(table, pairs.reshape(16, 512))
    up = relocate(acc_up[0], by_x + by_z)
    down = relocate(acc_down[0], by_z + by_x)
    new_up, new_down = pl.pallas_call(
        final_kernel,
        out_shape=[shape((D, HID_DEV), bf16), shape((HID_DEV, D), bf16)],
        in_specs=[VMEM] * 6,
        out_specs=[VMEM] * 2,
        compiler_params=PARAMS,
        name="final",
    )(up, down, own, recv, own_head, head)
    return new_up[None], new_down[None], loss[0, 0]


def solution(mesh):
    fine = Mesh(mesh.devices.reshape(4, 4, 4, 4, 2), ("x", "zl", "zh", "y", "c"))
    grp, ep = ("x", "zl"), ("zh", "y", "c")
    return jax.shard_map(
        body,
        mesh=fine,
        in_specs=(P(ep, None), P(ep, None), P(ep, None), P(), P(), P(), P())
        + (P(grp, None, ep), P(grp, ep, None)) * 2,
        out_specs=(P(grp, None, ep), P(grp, ep, None), P()),
        check_vma=False,
    )
```

```python
import functools

import jax
import jax.numpy as jnp
from jax import lax
from jax.experimental import pallas as pl
from jax.experimental.pallas import tpu as pltpu
from jax.sharding import Mesh
from jax.sharding import PartitionSpec as P

D = 2048
HID_DEV = 128
EXP_GRP = 4
TOK_DEV = 256
CAP = 48
WIDE = D + 128
ROWS = 16 * CAP
PAIRS = 4096

f32 = jnp.float32
bf16 = jnp.bfloat16
VMEM = pl.BlockSpec(memory_space=pltpu.VMEM)
SMEM = pl.BlockSpec(memory_space=pltpu.SMEM)
PARAMS = pltpu.CompilerParams(vmem_limit_bytes=48 * 1024 * 1024)
NT = (((1,), (1,)), ((), ()))

BLOCKS = [(EXP_GRP * CAP * d + CAP * k, k, d) for d in range(4) for k in range(EXP_GRP)]
SPACED = pl.CostEstimate(flops=10**11, bytes_accessed=0, transcendentals=0)
ANY = pl.BlockSpec(memory_space=pl.ANY)


def shape(dims, kind):
    return jax.ShapeDtypeStruct(dims, kind)


def iota(dims, axis):
    return lax.broadcasted_iota(jnp.int32, dims, axis)


def thirds(value):
    first = value.astype(bf16).astype(f32)
    second = (value - first).astype(bf16).astype(f32)
    third = (value - first - second).astype(bf16).astype(f32)
    return first, second, third


def weights_kernel(up_ref, down_ref, head_ref, out_ref):
    out_ref[:D, :] = up_ref[...]
    head = jnp.broadcast_to(head_ref[...], (16, D))
    proj = lax.dot_general(head, down_ref[...], NT, preferred_element_type=f32)
    first, second, third = thirds(proj)
    row = iota((16, HID_DEV), 0)
    packed = jnp.where(row == 0, first, jnp.where(row == 1, second, jnp.where(row == 2, third, 0.0)))
    out_ref[D:, :] = packed.astype(bf16)


def dispatch_kernel(group_ref, mask_ref, info_ref, tok_ref, routes_ref, gates_ref, pair_ref, head_ref, *outs):
    out_refs, base_ref = outs[:4], outs[4]
    grp, zh, member = info_ref[0], info_ref[1], info_ref[2]
    routes = routes_ref[...]
    gates = gates_ref[...]
    sel, gate = [], []
    for k in range(EXP_GRP):
        slot = zh ^ k
        mask = mask_ref[slot]
        expert = jnp.int32(0)
        for j in range(16):
            found = (group_ref[4 * j + slot] ^ mask) == grp
            expert = jnp.where(found, 4 * j + slot, expert)
        hit = routes == expert
        sel.append(jnp.sum(jnp.where(hit, 1.0, 0.0), axis=0, keepdims=True))
        gate.append(jnp.sum(jnp.where(hit, gates, 0.0), axis=0, keepdims=True))
    row8 = iota((8, TOK_DEV), 0)
    chosen = jnp.zeros((8, TOK_DEV), f32)
    for k in range(EXP_GRP):
        chosen = jnp.where(row8 == k, sel[k], chosen)
    tri = jnp.where(iota((TOK_DEV, TOK_DEV), 0) <= iota((TOK_DEV, TOK_DEV), 1), 1.0, 0.0).astype(bf16)
    place = jnp.dot(chosen.astype(bf16), tri, preferred_element_type=f32) - 1.0
    own = (iota((TOK_DEV, 1), 0) + member * TOK_DEV).astype(f32)

    def look(r, code):
        first = pair_ref[pl.ds(r, 1), :]
        second = pair_ref[pl.ds(r + 32, 1), :]
        return jnp.where(first == own, second + 1.0, jnp.where(second == own, -1.0 - first, code))

    code = lax.fori_loop(0, 32, look, jnp.zeros((TOK_DEV, 128), f32), unroll=4)
    code = jnp.sum(code, axis=1, keepdims=True)
    partner = jnp.abs(code) - 1.0
    high = jnp.floor(partner * (1.0 / TOK_DEV))
    low = partner - high * TOK_DEV
    lane = iota((TOK_DEV, 128), 1)
    by_token = jnp.where(lane == 13, high, jnp.where(lane == 14, low, jnp.where(lane == 15, jnp.where(code > 0, 1.0, -1.0), 0.0)))
    by_token = jnp.where(lane == 0, iota((TOK_DEV, 128), 0).astype(f32), by_token).astype(bf16)
    rows = iota((128, TOK_DEV), 0)
    by_slot = jnp.zeros((128, TOK_DEV), f32)
    for k in range(EXP_GRP):
        for j, part in enumerate(thirds(gate[k])):
            by_slot = jnp.where(rows == 1 + 3 * k + j, part, by_slot)
    by_slot = by_slot.astype(bf16)
    base_ref[...] = lax.dot_general(
        jnp.broadcast_to(head_ref[...], (16, D)), tok_ref[...], NT, preferred_element_type=f32
    )[:8]
    height = iota((CAP, TOK_DEV), 0).astype(f32)
    picks = [
        jnp.where((place[k : k + 1] == height) & (sel[k] > 0.5), 1.0, 0.0).astype(bf16) for k in range(EXP_GRP)
    ]
    pick = jnp.concatenate(picks, axis=0)
    notes = jnp.dot(pick, by_token, preferred_element_type=f32) + lax.dot_general(
        pick, by_slot, NT, preferred_element_type=f32
    )
    wide = jnp.dot(pick, tok_ref[...], preferred_element_type=f32)
    for k in range(EXP_GRP):
        out_refs[k][:, :D] = wide[CAP * k : CAP * (k + 1)].astype(bf16)
        out_refs[k][:, D:] = notes[CAP * k : CAP * (k + 1)].astype(bf16)


def forward_kernel(info_ref, base_ref, own_w_ref, other_w_ref, *refs):
    groups, (x_ref, slope_ref, hid_ref, note_ref, part_ref, u_ref) = refs[:4], refs[-6:]
    grp, zh, y = info_ref[0], info_ref[1], info_ref[3]
    u_ref[:, :HID_DEV] = own_w_ref[:D, :]
    u_ref[:, HID_DEV:] = other_w_ref[:D, :]
    start = 0
    for ref in groups:
        count = ref.shape[0]
        x_ref[start : start + count, :] = ref[:, :D]
        note_ref[start : start + count, :] = ref[:, D:].astype(f32)
        start += count
    pieces = jnp.concatenate([own_w_ref[D:, :], other_w_ref[D:, :]], axis=1).astype(f32)
    proj = pieces[0:1] + pieces[1:2] + pieces[2:3]
    pre = jnp.dot(x_ref[...], u_ref[...], preferred_element_type=f32)
    sig = jax.nn.sigmoid(pre)
    hidden = (pre * sig).astype(bf16)
    hid_ref[...] = hidden
    slope_ref[...] = proj * (sig * (1.0 + pre * (1.0 - sig)))
    value = jnp.sum(hidden.astype(f32) * proj, axis=1, keepdims=True)
    lane = iota((CAP, 128), 1)
    token = iota((CAP, TOK_DEV), 1).astype(f32)
    row = iota((16, TOK_DEV), 0)
    total = jnp.where((row == zh * 4 + y) & (grp == 0), base_ref[0:1, :], 0.0)
    for at, k, d in BLOCKS:
        note = note_ref[at : at + CAP, :]
        gate = jnp.sum(jnp.where((lane >= 1 + 3 * k) & (lane < 4 + 3 * k), note, 0.0), axis=1, keepdims=True)
        term = gate * value[at : at + CAP]
        spread = jnp.sum(jnp.where(note[:, 0:1] == token, term, 0.0), axis=0, keepdims=True)
        total = total + jnp.where(row == (zh ^ k) * 4 + (y ^ d), spread, 0.0)
    part_ref[...] = total


def backward_kernel(info_ref, table_ref, x_ref, slope_ref, hid_ref, note_ref, *refs):
    own_ref, send_ref, own_head_ref = refs[-3:]
    zh, c, y = info_ref[1], info_ref[4], info_ref[3]
    table = table_ref[...]
    note = note_ref[...]
    token = iota((CAP, TOK_DEV), 1).astype(f32)
    lane = iota((CAP, 128), 1)
    mine, gates = [], []
    for at, k, d in BLOCKS:
        block = ((zh ^ k) * 4 + (y ^ d)) * 2 + c
        values = table_ref[pl.ds(block, 1), :]
        part = note_ref[at : at + CAP, :]
        mine.append(jnp.sum(jnp.where(part[:, 0:1] == token, values, 0.0), axis=1, keepdims=True))
        gates.append(
            jnp.sum(jnp.where((lane >= 1 + 3 * k) & (lane < 4 + 3 * k), part, 0.0), axis=1, keepdims=True)
        )
    mine = jnp.concatenate(mine, axis=0)
    gate = jnp.concatenate(gates, axis=0)
    hot = jnp.where(iota((ROWS, 32), 1).astype(f32) == note[:, 13:14], 1.0, 0.0).astype(bf16)
    found = jnp.zeros((ROWS, TOK_DEV), f32)
    for part in thirds(table):
        found = found + jnp.dot(hot, part.astype(bf16), preferred_element_type=f32)
    places = iota((ROWS, TOK_DEV), 1).astype(f32)
    theirs = jnp.sum(jnp.where(places == note[:, 14:15], found, 0.0), axis=1, keepdims=True)
    side = note[:, 15:16]
    margin = side * (mine - theirs)
    grad = -side * (64.0 * jax.nn.sigmoid(-margin)) * gate
    hid_grad = jnp.sum(grad * hid_ref[...].astype(f32), axis=0, keepdims=True)
    pre_grad = (grad * slope_ref[...]).astype(bf16)
    out = lax.dot_general(x_ref[...], pre_grad, (((0,), (0,)), ((), ())), preferred_element_type=f32)
    own_ref[...] = out[:, :HID_DEV]
    send_ref[:D, :] = out[:, HID_DEV:]
    own_head_ref[...] = jnp.broadcast_to(hid_grad[:, :HID_DEV], (8, HID_DEV))
    send_ref[D:, :] = jnp.broadcast_to(hid_grad[:, HID_DEV:], (8, HID_DEV))


def loss_kernel(table_ref, pair_ref, out_ref):
    parts = jnp.concatenate([p.astype(bf16) for p in thirds(table_ref[...])], axis=0)

    def rewards_of(index):
        high = jnp.floor(index * (1.0 / TOK_DEV))
        low = index - high * TOK_DEV
        count = index.shape[1]
        row = iota((96, count), 0) & 31
        hot = jnp.where(row.astype(f32) == high, 1.0, 0.0).astype(bf16)
        found = lax.dot_general(parts, hot, (((0,), (0,)), ((), ())), preferred_element_type=f32)
        return jnp.sum(jnp.where(iota((TOK_DEV, count), 0).astype(f32) == low, found, 0.0), axis=0, keepdims=True)

    def step(r, total):
        margin = rewards_of(pair_ref[pl.ds(r, 1), :]) - rewards_of(pair_ref[pl.ds(r + 8, 1), :])
        return total + jnp.maximum(-margin, 0.0) + jnp.log1p(jnp.exp(-jnp.abs(margin)))

    total = lax.fori_loop(0, 8, step, jnp.zeros((1, 512), f32))
    out_ref[...] = jnp.broadcast_to(jnp.sum(total, axis=1, keepdims=True) * (1.0 / PAIRS), (1, 128))


def final_kernel(up_ref, down_ref, own_ref, recv_ref, own_head_ref, head_ref, new_up_ref, new_down_ref):
    new_up_ref[...] = (up_ref[...].astype(f32) + (own_ref[...] + recv_ref[:D, :])).astype(bf16)
    grad = own_head_ref[0:1] + recv_ref[D : D + 1, :]
    square = (HID_DEV, HID_DEV)
    column = jnp.sum(jnp.where(iota(square, 0) == iota(square, 1), grad, 0.0), axis=1, keepdims=True)
    for j in range(D // HID_DEV):
        at = j * HID_DEV
        old = down_ref[at : at + HID_DEV, :].astype(f32)
        step = column * head_ref[:, at : at + HID_DEV].astype(f32)
        new_down_ref[:, at : at + HID_DEV] = (old + step).astype(bf16)


def pack_kernel(up_ref, down_ref, earlier_ref, out_ref):
    out_ref[:D, :] = up_ref[...]
    for j in range(D // HID_DEV):
        at = j * HID_DEV
        out_ref[D + at : D + at + HID_DEV, :] = down_ref[:, at : at + HID_DEV]


def pick_kernel(outs, take_ref, got_ref, own_ref, *refs):
    for wanted, ref in ((1, got_ref), (0, own_ref)):

        @pl.when(take_ref[0] == wanted)
        def _(ref=ref):
            at = 0
            for out_ref in refs[-outs:]:
                count = out_ref.shape[0]
                out_ref[...] = ref[at : at + count, :]
                at += count


def join_kernel(*refs):
    for k in range(EXP_GRP):
        refs[-1][CAP * k : CAP * (k + 1), :] = refs[k][...]


def swap(block, axis, mask):
    count = lax.axis_size(axis)
    return lax.ppermute(block, axis, [(i, i ^ mask) for i in range(count)])


def pick(stage, got, own, *earlier, outs=1):
    out = shape((own.shape[0] // outs, own.shape[1]), own.dtype)
    picked = pl.pallas_call(
        functools.partial(pick_kernel, outs),
        out_shape=[out] * outs,
        in_specs=[SMEM, VMEM, VMEM] + [ANY] * len(earlier),
        out_specs=[VMEM] * outs,
        compiler_params=PARAMS,
        cost_estimate=SPACED,
        name="pick",
    )(stage[2], got, own, *earlier)
    return picked if outs > 1 else picked[0]


def join(blocks, *earlier):
    return pl.pallas_call(
        join_kernel,
        out_shape=shape((EXP_GRP * CAP, WIDE), bf16),
        in_specs=[VMEM] * EXP_GRP + [ANY] * len(earlier),
        out_specs=VMEM,
        compiler_params=PARAMS,
        cost_estimate=SPACED,
        name="join",
    )(*blocks, *earlier)


def body(tokens, routes, gate_values, old_group, move_mask, pair_index, reward_head, w_up, w_down, acc_up, acc_down):
    x, zl, zh, y, c = (lax.axis_index(a) for a in ("x", "zl", "zh", "y", "c"))
    info = jnp.stack([x * 4 + zl, zh, zh * 8 + y * 2 + c, y, c]).astype(jnp.int32)
    head = reward_head.reshape(1, D)
    mask = jnp.sum(jnp.where(jnp.arange(EXP_GRP) == zh, move_mask, 0))
    bit = [jnp.bitwise_and(jnp.right_shift(mask, i), 1) for i in range(4)]
    x1 = ("x", 1, jnp.bitwise_xor(bit[2], bit[3]).reshape(1))
    x3 = ("x", 3, bit[3].reshape(1))
    z1 = ("zl", 1, bit[0].reshape(1))
    z2 = ("zl", 2, bit[1].reshape(1))

    weights = pl.pallas_call(
        weights_kernel,
        out_shape=shape((D + 16, HID_DEV), bf16),
        in_specs=[VMEM] * 3,
        out_specs=VMEM,
        compiler_params=PARAMS,
        name="weights",
    )(w_up[0], w_down[0], head)
    got = swap(weights, *z1[:2])

    pairs = pair_index.astype(f32)
    *sent, base = pl.pallas_call(
        dispatch_kernel,
        out_shape=[shape((CAP, WIDE), bf16)] * 4 + [shape((8, TOK_DEV), f32)],
        in_specs=[SMEM] * 3 + [VMEM] * 5,
        out_specs=[VMEM] * 5,
        compiler_params=PARAMS,
        name="dispatch",
    )(old_group, move_mask, info, tokens, routes.T, gate_values.T, pairs.reshape(64, 128), head)
    blocks = [sent[0], swap(sent[1], "zh", 1), swap(sent[2], "zh", 2), swap(sent[3], "zh", 3)]
    accums = pl.pallas_call(
        pack_kernel,
        out_shape=shape((2 * D, HID_DEV), bf16),
        in_specs=[VMEM, VMEM, ANY],
        out_specs=VMEM,
        compiler_params=PARAMS,
        cost_estimate=SPACED,
        name="pack",
    )(acc_up[0], acc_down[0], sent[0])
    acc_got = swap(accums, *x1[:2])

    weights = pick(z1, got, weights, accums)
    got = swap(weights, *x1[:2])
    weights = pick(x1, got, weights)
    got = swap(weights, *x3[:2])
    rows = join(blocks, weights)
    held = [rows] + [swap(rows, "y", d) for d in (1, 2, 3)]
    accums = pick(x1, acc_got, accums, rows)
    acc_got = swap(accums, *x3[:2])
    weights = pick(x3, got, weights, accums)
    got = swap(weights, *z2[:2])
    up, down = pick(x3, acc_got, accums, weights, outs=2)
    up_got = swap(up, *z1[:2])
    down_got = swap(down, *z2[:2])
    weights = pick(z2, got, weights, up)
    other_weights = swap(weights, "c", 1)

    xs, slope, hidden, notes, part = pl.pallas_call(
        forward_kernel,
        out_shape=[
            shape((ROWS, D), bf16),
            shape((ROWS, 2 * HID_DEV), f32),
            shape((ROWS, 2 * HID_DEV), bf16),
            shape((ROWS, 128), f32),
            shape((16, TOK_DEV), f32),
        ],
        in_specs=[SMEM] + [VMEM] * 7,
        out_specs=[VMEM] * 5,
        scratch_shapes=[pltpu.VMEM((D, 2 * HID_DEV), bf16)],
        compiler_params=PARAMS,
        name="forward",
    )(info, base, weights, other_weights, *held)

    mine = lax.all_to_all(part, ("x", "y"), 0, 0, tiled=True)
    mine = jnp.broadcast_to(jnp.sum(mine, axis=0, keepdims=True), (16, TOK_DEV))
    mine = lax.all_to_all(mine, ("zl", "zh"), 0, 0, tiled=True)
    mine = jnp.broadcast_to(jnp.sum(mine, axis=0, keepdims=True), (32, TOK_DEV))
    up = pick(z1, up_got, up, mine)
    up_got = swap(up, *z2[:2])
    down = pick(z2, down_got, down, mine)
    down_got = swap(down, *z1[:2])
    table = lax.all_to_all(mine, ("x", "y", "c"), 0, 0, tiled=True)

    own, send, own_head = pl.pallas_call(
        backward_kernel,
        out_shape=[shape((D, HID_DEV), f32), shape((D + 8, HID_DEV), f32), shape((8, HID_DEV), f32)],
        in_specs=[SMEM] + [VMEM] * 5 + [ANY] * 2,
        out_specs=[VMEM] * 3,
        compiler_params=PARAMS,
        name="backward",
    )(info, table, xs, slope, hidden, notes, up, down)
    recv = swap(send, "c", 1)
    loss = pl.pallas_call(
        loss_kernel,
        out_shape=shape((1, 128), f32),
        in_specs=[VMEM] * 2,
        out_specs=VMEM,
        compiler_params=PARAMS,
        name="loss",
    )(table, pairs.reshape(16, 512))
    up = pick(z2, up_got, up)
    down = pick(z1, down_got, down)
    new_up, new_down = pl.pallas_call(
        final_kernel,
        out_shape=[shape((D, HID_DEV), bf16), shape((HID_DEV, D), bf16)],
        in_specs=[VMEM] * 6,
        out_specs=[VMEM] * 2,
        compiler_params=PARAMS,
        name="final",
    )(up, down, own, recv, own_head, head)
    return new_up[None], new_down[None], loss[0, 0]


def solution(mesh):
    fine = Mesh(mesh.devices.reshape(4, 4, 4, 4, 2), ("x", "zl", "zh", "y", "c"))
    grp, ep = ("x", "zl"), ("zh", "y", "c")
    return jax.shard_map(
        body,
        mesh=fine,
        in_specs=(P(ep, None), P(ep, None), P(ep, None), P(), P(), P(), P())
        + (P(grp, None, ep), P(grp, ep, None)) * 2,
        out_specs=(P(grp, None, ep), P(grp, ep, None), P()),
        check_vma=False,
    )
```

```python
import functools

import jax
import jax.numpy as jnp
from jax import lax
from jax.experimental import pallas as pl
from jax.experimental.pallas import tpu as pltpu
from jax.sharding import Mesh
from jax.sharding import PartitionSpec as P

D = 2048
HID_DEV = 128
EXP_GRP = 4
TOK_DEV = 256
CAP = 48
WIDE = D + 128
ROWS = 16 * CAP
PAIRS = 4096

f32 = jnp.float32
bf16 = jnp.bfloat16
VMEM = pl.BlockSpec(memory_space=pltpu.VMEM)
SMEM = pl.BlockSpec(memory_space=pltpu.SMEM)
PARAMS = pltpu.CompilerParams(vmem_limit_bytes=24 * 1024 * 1024)
NT = (((1,), (1,)), ((), ()))

BLOCKS = [(EXP_GRP * CAP * d + CAP * k, k, d) for d in range(4) for k in range(EXP_GRP)]
SPACED = pl.CostEstimate(flops=10**11, bytes_accessed=0, transcendentals=0)
ANY = pl.BlockSpec(memory_space=pl.ANY)


def shape(dims, kind):
    return jax.ShapeDtypeStruct(dims, kind)


def iota(dims, axis):
    return lax.broadcasted_iota(jnp.int32, dims, axis)


def thirds(value):
    first = value.astype(bf16).astype(f32)
    second = (value - first).astype(bf16).astype(f32)
    third = (value - first - second).astype(bf16).astype(f32)
    return first, second, third


def dispatch_kernel(
    group_ref,
    mask_ref,
    info_ref,
    tok_ref,
    routes_ref,
    gates_ref,
    pair_ref,
    head_ref,
    up_ref,
    down_ref,
    acc_up_ref,
    acc_down_ref,
    *outs,
):
    out_refs, (base_ref, weights_ref, acc_ref) = outs[:4], outs[4:]
    acc_ref[:D, :] = acc_up_ref[...]
    for j in range(D // HID_DEV):
        at = j * HID_DEV
        acc_ref[D + at : D + at + HID_DEV, :] = acc_down_ref[:, at : at + HID_DEV]
    weights_ref[:D, :] = up_ref[...]
    head = head_ref[...].astype(f32)
    head = jnp.concatenate([head[j : j + 1] for j in range(D // 128)], axis=1)
    head = jnp.broadcast_to(head, (16, D)).astype(bf16)
    proj = lax.dot_general(head, down_ref[...], NT, preferred_element_type=f32)
    first, second, third = thirds(proj)
    row = iota((16, HID_DEV), 0)
    packed = jnp.where(row == 0, first, jnp.where(row == 1, second, jnp.where(row == 2, third, 0.0)))
    weights_ref[D:, :] = packed.astype(bf16)
    grp, zh, member = info_ref[0], info_ref[1], info_ref[2]
    routes = routes_ref[...]
    gates = gates_ref[...]
    sel, gate = [], []
    for k in range(EXP_GRP):
        slot = zh ^ k
        mask = mask_ref[slot]
        expert = jnp.int32(0)
        for j in range(16):
            found = (group_ref[4 * j + slot] ^ mask) == grp
            expert = jnp.where(found, 4 * j + slot, expert)
        hit = routes == expert
        sel.append(jnp.sum(jnp.where(hit, 1.0, 0.0), axis=0, keepdims=True))
        gate.append(jnp.sum(jnp.where(hit, gates, 0.0), axis=0, keepdims=True))
    row8 = iota((8, TOK_DEV), 0)
    chosen = jnp.zeros((8, TOK_DEV), f32)
    for k in range(EXP_GRP):
        chosen = jnp.where(row8 == k, sel[k], chosen)
    tri = jnp.where(iota((TOK_DEV, TOK_DEV), 0) <= iota((TOK_DEV, TOK_DEV), 1), 1.0, 0.0).astype(bf16)
    place = jnp.dot(chosen.astype(bf16), tri, preferred_element_type=f32) - 1.0
    own = (iota((TOK_DEV, 1), 0) + member * TOK_DEV).astype(f32)

    def look(r, code):
        first = pair_ref[pl.ds(r, 1), :].astype(f32)
        second = pair_ref[pl.ds(r + 32, 1), :].astype(f32)
        return jnp.where(first == own, second + 1.0, jnp.where(second == own, -1.0 - first, code))

    code = lax.fori_loop(0, 32, look, jnp.zeros((TOK_DEV, 128), f32), unroll=4)
    code = jnp.sum(code, axis=1, keepdims=True)
    partner = jnp.abs(code) - 1.0
    high = jnp.floor(partner * (1.0 / TOK_DEV))
    low = partner - high * TOK_DEV
    lane = iota((TOK_DEV, 128), 1)
    by_token = jnp.where(lane == 13, high, jnp.where(lane == 14, low, jnp.where(lane == 15, jnp.where(code > 0, 1.0, -1.0), 0.0)))
    by_token = jnp.where(lane == 0, iota((TOK_DEV, 128), 0).astype(f32), by_token).astype(bf16)
    rows = iota((128, TOK_DEV), 0)
    by_slot = jnp.zeros((128, TOK_DEV), f32)
    for k in range(EXP_GRP):
        for j, part in enumerate(thirds(gate[k])):
            by_slot = jnp.where(rows == 1 + 3 * k + j, part, by_slot)
    by_slot = by_slot.astype(bf16)
    base_ref[...] = lax.dot_general(head, tok_ref[...], NT, preferred_element_type=f32)[:8]
    height = iota((CAP, TOK_DEV), 0).astype(f32)
    picks = [
        jnp.where((place[k : k + 1] == height) & (sel[k] > 0.5), 1.0, 0.0).astype(bf16) for k in range(EXP_GRP)
    ]
    pick = jnp.concatenate(picks, axis=0)
    notes = jnp.dot(pick, by_token, preferred_element_type=f32) + lax.dot_general(
        pick, by_slot, NT, preferred_element_type=f32
    )
    wide = jnp.dot(pick, tok_ref[...], preferred_element_type=f32)
    for k in range(EXP_GRP):
        out_refs[k][:, :D] = wide[CAP * k : CAP * (k + 1)].astype(bf16)
        out_refs[k][:, D:] = notes[CAP * k : CAP * (k + 1)].astype(bf16)


def forward_kernel(info_ref, base_ref, own_w_ref, other_w_ref, *refs):
    groups, (x_ref, keep_ref, part_ref, u_ref) = refs[:4], refs[-4:]
    grp, zh, y = info_ref[0], info_ref[1], info_ref[3]
    u_ref[:, :HID_DEV] = own_w_ref[:D, :]
    u_ref[:, HID_DEV:] = other_w_ref[:D, :]
    start = 0
    for ref in groups:
        count = ref.shape[0]
        x_ref[start : start + count, :] = ref[:, :D]
        keep_ref[start : start + count, 2 * HID_DEV :] = ref[:, D:].astype(f32)
        start += count
    pieces = jnp.concatenate([own_w_ref[D:, :], other_w_ref[D:, :]], axis=1).astype(f32)
    proj = pieces[0:1] + pieces[1:2] + pieces[2:3]
    pre = jnp.dot(x_ref[...], u_ref[...], preferred_element_type=f32)
    sig = jax.nn.sigmoid(pre)
    hidden = (pre * sig).astype(bf16)
    keep_ref[:ROWS, : 2 * HID_DEV] = pre
    keep_ref[ROWS:, : 2 * HID_DEV] = jnp.broadcast_to(proj, (8, 2 * HID_DEV))
    value = jnp.sum(hidden.astype(f32) * proj, axis=1, keepdims=True)
    lane = iota((CAP, 128), 1)
    token = iota((CAP, TOK_DEV), 1).astype(f32)
    row = iota((16, TOK_DEV), 0)
    total = jnp.where((row == zh * 4 + y) & (grp == 0), base_ref[0:1, :], 0.0)
    for at, k, d in BLOCKS:
        note = keep_ref[at : at + CAP, 2 * HID_DEV :]
        gate = jnp.sum(jnp.where((lane >= 1 + 3 * k) & (lane < 4 + 3 * k), note, 0.0), axis=1, keepdims=True)
        term = gate * value[at : at + CAP]
        spread = jnp.sum(jnp.where(note[:, 0:1] == token, term, 0.0), axis=0, keepdims=True)
        total = total + jnp.where(row == (zh ^ k) * 4 + (y ^ d), spread, 0.0)
    part_ref[...] = total


def backward_kernel(info_ref, table_ref, x_ref, keep_ref, own_ref, send_ref, own_head_ref):
    zh, c, y = info_ref[1], info_ref[4], info_ref[3]
    table = table_ref[...]
    note = keep_ref[:ROWS, 2 * HID_DEV :]
    token = iota((CAP, TOK_DEV), 1).astype(f32)
    lane = iota((CAP, 128), 1)
    mine, gates = [], []
    for at, k, d in BLOCKS:
        block = ((zh ^ k) * 4 + (y ^ d)) * 2 + c
        values = table_ref[pl.ds(block, 1), :]
        part = keep_ref[at : at + CAP, 2 * HID_DEV :]
        mine.append(jnp.sum(jnp.where(part[:, 0:1] == token, values, 0.0), axis=1, keepdims=True))
        gates.append(
            jnp.sum(jnp.where((lane >= 1 + 3 * k) & (lane < 4 + 3 * k), part, 0.0), axis=1, keepdims=True)
        )
    mine = jnp.concatenate(mine, axis=0)
    gate = jnp.concatenate(gates, axis=0)
    hot = jnp.where(iota((ROWS, 32), 1).astype(f32) == note[:, 13:14], 1.0, 0.0).astype(bf16)
    found = jnp.zeros((ROWS, TOK_DEV), f32)
    for part in thirds(table):
        found = found + jnp.dot(hot, part.astype(bf16), preferred_element_type=f32)
    places = iota((ROWS, TOK_DEV), 1).astype(f32)
    theirs = jnp.sum(jnp.where(places == note[:, 14:15], found, 0.0), axis=1, keepdims=True)
    side = note[:, 15:16]
    margin = side * (mine - theirs)
    grad = -side * (64.0 * jax.nn.sigmoid(-margin)) * gate
    pre = keep_ref[:ROWS, : 2 * HID_DEV]
    proj = keep_ref[ROWS : ROWS + 1, : 2 * HID_DEV]
    sig = jax.nn.sigmoid(pre)
    hidden = (pre * sig).astype(bf16).astype(f32)
    hid_grad = jnp.sum(grad * hidden, axis=0, keepdims=True)
    pre_grad = (grad * proj * (sig * (1.0 + pre * (1.0 - sig)))).astype(bf16)
    out = lax.dot_general(x_ref[...], pre_grad, (((0,), (0,)), ((), ())), preferred_element_type=f32)
    own_ref[...] = out[:, :HID_DEV]
    send_ref[:D, :] = out[:, HID_DEV:]
    own_head_ref[...] = jnp.broadcast_to(hid_grad[:, :HID_DEV], (8, HID_DEV))
    send_ref[D:, :] = jnp.broadcast_to(hid_grad[:, HID_DEV:], (8, HID_DEV))


def loss_kernel(table_ref, pair_ref, out_ref):
    parts = jnp.concatenate([p.astype(bf16) for p in thirds(table_ref[...])], axis=0)

    def rewards_of(index):
        high = jnp.floor(index * (1.0 / TOK_DEV))
        low = index - high * TOK_DEV
        count = index.shape[1]
        row = iota((96, count), 0) & 31
        hot = jnp.where(row.astype(f32) == high, 1.0, 0.0).astype(bf16)
        found = lax.dot_general(parts, hot, (((0,), (0,)), ((), ())), preferred_element_type=f32)
        return jnp.sum(jnp.where(iota((TOK_DEV, count), 0).astype(f32) == low, found, 0.0), axis=0, keepdims=True)

    def step(r, total):
        def line(at):
            rows = [pair_ref[pl.ds(at + i, 1), :].astype(f32) for i in range(4)]
            return jnp.concatenate(rows, axis=1)

        margin = rewards_of(line(4 * r)) - rewards_of(line(4 * r + 32))
        return total + jnp.maximum(-margin, 0.0) + jnp.log1p(jnp.exp(-jnp.abs(margin)))

    total = lax.fori_loop(0, 8, step, jnp.zeros((1, 512), f32))
    out_ref[...] = jnp.broadcast_to(jnp.sum(total, axis=1, keepdims=True) * (1.0 / PAIRS), (1, 128))


def final_kernel(take_ref, acc_ref, got_ref, own_ref, recv_ref, own_head_ref, head_ref, new_up_ref, new_down_ref):
    step = own_ref[...] + recv_ref[:D, :]
    grad = own_head_ref[0:1] + recv_ref[D : D + 1, :]
    square = (HID_DEV, HID_DEV)
    column = jnp.sum(jnp.where(iota(square, 0) == iota(square, 1), grad, 0.0), axis=1, keepdims=True)
    head = head_ref[...].astype(f32)
    for wanted, ref in ((1, got_ref), (0, acc_ref)):

        @pl.when(take_ref[0] == wanted)
        def _(ref=ref):
            new_up_ref[...] = (ref[:D, :].astype(f32) + step).astype(bf16)
            for j in range(D // HID_DEV):
                at = j * HID_DEV
                old = ref[D + at : D + at + HID_DEV, :].astype(f32)
                new_down_ref[:, at : at + HID_DEV] = (old + column * head[j : j + 1]).astype(bf16)


def pick_kernel(count, take_ref, *refs):
    got_refs, own_refs, out_refs = refs[:count], refs[count : 2 * count], refs[-count:]
    for i in range(count):

        @pl.when(take_ref[i] == 1)
        def _(i=i):
            out_refs[i][...] = got_refs[i][...]

        @pl.when(take_ref[i] == 0)
        def _(i=i):
            out_refs[i][...] = own_refs[i][...]


def join_kernel(*refs):
    for k in range(EXP_GRP):
        refs[-1][CAP * k : CAP * (k + 1), :] = refs[k][...]


def swap(block, axis, mask):
    count = lax.axis_size(axis)
    return lax.ppermute(block, axis, [(i, i ^ mask) for i in range(count)])


def picks(stages, got, own, *earlier):
    count = len(stages)
    return pl.pallas_call(
        functools.partial(pick_kernel, count),
        out_shape=[shape(o.shape, o.dtype) for o in own],
        in_specs=[SMEM] + [VMEM] * (2 * count) + [ANY] * len(earlier),
        out_specs=[VMEM] * count,
        compiler_params=PARAMS,
        cost_estimate=SPACED,
        name="pick",
    )(jnp.concatenate([s[2] for s in stages]), *got, *own, *earlier)


def pick(stage, got, own, *earlier):
    return picks([stage], [got], [own], *earlier)[0]


def join(blocks, *earlier):
    return pl.pallas_call(
        join_kernel,
        out_shape=shape((EXP_GRP * CAP, WIDE), bf16),
        in_specs=[VMEM] * EXP_GRP + [ANY] * len(earlier),
        out_specs=VMEM,
        compiler_params=PARAMS,
        cost_estimate=SPACED,
        name="join",
    )(*blocks, *earlier)


def body(tokens, routes, gate_values, old_group, move_mask, pair_index, reward_head, w_up, w_down, acc_up, acc_down):
    x, zl, zh, y, c = (lax.axis_index(a) for a in ("x", "zl", "zh", "y", "c"))
    info = jnp.stack([x * 4 + zl, zh, zh * 8 + y * 2 + c, y, c]).astype(jnp.int32)
    head = reward_head.reshape(D // 128, 128)
    pairs = pair_index.reshape(64, 128)
    mask = jnp.sum(jnp.where(jnp.arange(EXP_GRP) == zh, move_mask, 0))
    bit = [jnp.bitwise_and(jnp.right_shift(mask, i), 1) for i in range(4)]
    x1 = ("x", 1, jnp.bitwise_xor(bit[2], bit[3]).reshape(1))
    x3 = ("x", 3, bit[3].reshape(1))
    z1 = ("zl", 1, bit[0].reshape(1))
    z2 = ("zl", 2, bit[1].reshape(1))

    *sent, base, weights, accums = pl.pallas_call(
        dispatch_kernel,
        out_shape=[shape((CAP, WIDE), bf16)] * 4 + [shape((8, TOK_DEV), f32), shape((D + 16, HID_DEV), bf16), shape((2 * D, HID_DEV), bf16)],
        in_specs=[SMEM] * 3 + [VMEM] * 9,
        out_specs=[VMEM] * 7,
        compiler_params=pltpu.CompilerParams(vmem_limit_bytes=63 * 1024 * 1024),
        name="dispatch",
    )(
        old_group,
        move_mask,
        info,
        tokens,
        routes.T,
        gate_values.T,
        pairs,
        head,
        w_up[0],
        w_down[0],
        acc_up[0],
        acc_down[0],
    )
    blocks = [sent[0], swap(sent[1], "zh", 1), swap(sent[2], "zh", 2), swap(sent[3], "zh", 3)]
    got = swap(weights, *x1[:2])
    acc_got = swap(accums, *x1[:2])
    weights = pick(x1, got, weights)
    got = swap(weights, *x3[:2])
    accums = pick(x1, acc_got, accums, weights)
    acc_got = swap(accums, *x3[:2])
    weights = pick(x3, got, weights, accums)
    got = swap(weights, *z1[:2])
    rows = join(blocks, weights)
    held = [rows] + [swap(rows, "y", d) for d in (1, 2, 3)]
    weights = pick(z1, got, weights, rows)
    got = swap(weights, *z2[:2])
    accums = pick(x3, acc_got, accums, weights)
    acc_got = swap(accums, *z1[:2])
    weights = pick(z2, got, weights, accums)
    other_weights = swap(weights, "c", 1)

    xs, keep, part = pl.pallas_call(
        forward_kernel,
        out_shape=[
            shape((ROWS, D), bf16),
            shape((ROWS + 8, 2 * HID_DEV + 128), f32),
            shape((16, TOK_DEV), f32),
        ],
        in_specs=[SMEM] + [VMEM] * 7,
        out_specs=[VMEM] * 3,
        scratch_shapes=[pltpu.VMEM((D, 2 * HID_DEV), bf16)],
        compiler_params=PARAMS,
        name="forward",
    )(info, base, weights, other_weights, *held)

    accums = pick(z1, acc_got, accums, part)
    part, accums = lax.optimization_barrier((part, accums))
    acc_got = swap(accums, *z2[:2])
    mine = lax.all_to_all(part, ("x", "y"), 0, 0, tiled=True)
    mine = jnp.broadcast_to(jnp.sum(mine, axis=0, keepdims=True), (16, TOK_DEV))
    mine = lax.all_to_all(mine, ("zl", "zh"), 0, 0, tiled=True)
    mine = jnp.broadcast_to(jnp.sum(mine, axis=0, keepdims=True), (32, TOK_DEV))
    table = lax.all_to_all(mine, ("x", "y", "c"), 0, 0, tiled=True)

    table, acc_got = lax.optimization_barrier((table, acc_got))
    own, send, own_head = pl.pallas_call(
        backward_kernel,
        out_shape=[shape((D, HID_DEV), f32), shape((D + 8, HID_DEV), f32), shape((8, HID_DEV), f32)],
        in_specs=[SMEM] + [VMEM] * 3,
        out_specs=[VMEM] * 3,
        compiler_params=PARAMS,
        cost_estimate=SPACED,
        name="backward",
    )(info, table, xs, keep)
    recv = swap(send, "c", 1)
    loss = pl.pallas_call(
        loss_kernel,
        out_shape=shape((1, 128), f32),
        in_specs=[VMEM] * 2,
        out_specs=VMEM,
        compiler_params=PARAMS,
        cost_estimate=SPACED,
        name="loss",
    )(table, pairs)
    new_up, new_down = pl.pallas_call(
        final_kernel,
        out_shape=[shape((D, HID_DEV), bf16), shape((HID_DEV, D), bf16)],
        in_specs=[SMEM] + [VMEM] * 6,
        out_specs=[VMEM] * 2,
        compiler_params=PARAMS,
        name="final",
    )(z2[2], accums, acc_got, own, recv, own_head, head)
    return new_up[None], new_down[None], loss[0, 0]


def solution(mesh):
    fine = Mesh(mesh.devices.reshape(4, 4, 4, 4, 2), ("x", "zl", "zh", "y", "c"))
    grp, ep = ("x", "zl"), ("zh", "y", "c")
    return jax.shard_map(
        body,
        mesh=fine,
        in_specs=(P(ep, None), P(ep, None), P(ep, None), P(), P(), P(), P())
        + (P(grp, None, ep), P(grp, ep, None)) * 2,
        out_specs=(P(grp, None, ep), P(grp, ep, None), P()),
        check_vma=False,
    )
```

```python
import functools

import jax
import jax.numpy as jnp
from jax import lax
from jax.experimental import pallas as pl
from jax.experimental.pallas import tpu as pltpu
from jax.sharding import Mesh
from jax.sharding import PartitionSpec as P

D = 2048
HID_DEV = 128
EXP_GRP = 4
TOK_DEV = 256
CAP = 48
WIDE = D + 128
ROWS = 16 * CAP
PAIRS = 4096

f32 = jnp.float32
bf16 = jnp.bfloat16
VMEM = pl.BlockSpec(memory_space=pltpu.VMEM)
SMEM = pl.BlockSpec(memory_space=pltpu.SMEM)
PARAMS = pltpu.CompilerParams(vmem_limit_bytes=24 * 1024 * 1024)
NT = (((1,), (1,)), ((), ()))

BLOCKS = [(EXP_GRP * CAP * d + CAP * k, k, d) for d in range(4) for k in range(EXP_GRP)]
SPACED = pl.CostEstimate(flops=10**11, bytes_accessed=0, transcendentals=0)
ANY = pl.BlockSpec(memory_space=pl.ANY)


def shape(dims, kind):
    return jax.ShapeDtypeStruct(dims, kind)


def iota(dims, axis):
    return lax.broadcasted_iota(jnp.int32, dims, axis)


def thirds(value):
    first = value.astype(bf16).astype(f32)
    second = (value - first).astype(bf16).astype(f32)
    third = (value - first - second).astype(bf16).astype(f32)
    return first, second, third


def dispatch_kernel(
    group_ref,
    mask_ref,
    info_ref,
    tok_ref,
    routes_ref,
    gates_ref,
    pair_ref,
    head_ref,
    up_ref,
    down_ref,
    acc_up_ref,
    acc_down_ref,
    *outs,
):
    out_refs, (base_ref, weights_ref, acc_ref) = outs[:4], outs[4:]
    acc_ref[:D, :] = acc_up_ref[...]
    for j in range(D // HID_DEV):
        at = j * HID_DEV
        acc_ref[D + at : D + at + HID_DEV, :] = acc_down_ref[:, at : at + HID_DEV]
    weights_ref[:D, :] = up_ref[...]
    head = head_ref[...].astype(f32)
    head = jnp.concatenate([head[j : j + 1] for j in range(D // 128)], axis=1)
    head = jnp.broadcast_to(head, (16, D)).astype(bf16)
    proj = lax.dot_general(head, down_ref[...], NT, preferred_element_type=f32)
    first, second, third = thirds(proj)
    row = iota((16, HID_DEV), 0)
    packed = jnp.where(row == 0, first, jnp.where(row == 1, second, jnp.where(row == 2, third, 0.0)))
    weights_ref[D:, :] = packed.astype(bf16)
    grp, zh, member = info_ref[0], info_ref[1], info_ref[2]
    routes = routes_ref[...]
    gates = gates_ref[...]
    sel, gate = [], []
    for k in range(EXP_GRP):
        slot = zh ^ k
        mask = mask_ref[slot]
        expert = jnp.int32(0)
        for j in range(16):
            found = (group_ref[4 * j + slot] ^ mask) == grp
            expert = jnp.where(found, 4 * j + slot, expert)
        hit = routes == expert
        sel.append(jnp.sum(jnp.where(hit, 1.0, 0.0), axis=0, keepdims=True))
        gate.append(jnp.sum(jnp.where(hit, gates, 0.0), axis=0, keepdims=True))
    row8 = iota((8, TOK_DEV), 0)
    chosen = jnp.zeros((8, TOK_DEV), f32)
    for k in range(EXP_GRP):
        chosen = jnp.where(row8 == k, sel[k], chosen)
    tri = jnp.where(iota((TOK_DEV, TOK_DEV), 0) <= iota((TOK_DEV, TOK_DEV), 1), 1.0, 0.0).astype(bf16)
    place = jnp.dot(chosen.astype(bf16), tri, preferred_element_type=f32) - 1.0
    own = (iota((TOK_DEV, 1), 0) + member * TOK_DEV).astype(f32)

    def look(r, code):
        first = pair_ref[pl.ds(r, 1), :].astype(f32)
        second = pair_ref[pl.ds(r + 32, 1), :].astype(f32)
        return jnp.where(first == own, second + 1.0, jnp.where(second == own, -1.0 - first, code))

    code = lax.fori_loop(0, 32, look, jnp.zeros((TOK_DEV, 128), f32), unroll=4)
    code = jnp.sum(code, axis=1, keepdims=True)
    partner = jnp.abs(code) - 1.0
    high = jnp.floor(partner * (1.0 / TOK_DEV))
    low = partner - high * TOK_DEV
    lane = iota((TOK_DEV, 128), 1)
    by_token = jnp.where(lane == 13, high, jnp.where(lane == 14, low, jnp.where(lane == 15, jnp.where(code > 0, 1.0, -1.0), 0.0)))
    by_token = jnp.where(lane == 0, iota((TOK_DEV, 128), 0).astype(f32), by_token).astype(bf16)
    rows = iota((128, TOK_DEV), 0)
    by_slot = jnp.zeros((128, TOK_DEV), f32)
    for k in range(EXP_GRP):
        for j, part in enumerate(thirds(gate[k])):
            by_slot = jnp.where(rows == 1 + 3 * k + j, part, by_slot)
    by_slot = by_slot.astype(bf16)
    base_ref[...] = lax.dot_general(head, tok_ref[...], NT, preferred_element_type=f32)[:8]
    height = iota((CAP, TOK_DEV), 0).astype(f32)
    picks = [
        jnp.where((place[k : k + 1] == height) & (sel[k] > 0.5), 1.0, 0.0).astype(bf16) for k in range(EXP_GRP)
    ]
    pick = jnp.concatenate(picks, axis=0)
    notes = jnp.dot(pick, by_token, preferred_element_type=f32) + lax.dot_general(
        pick, by_slot, NT, preferred_element_type=f32
    )
    wide = jnp.dot(pick, tok_ref[...], preferred_element_type=f32)
    for k in range(EXP_GRP):
        out_refs[k][:, :D] = wide[CAP * k : CAP * (k + 1)].astype(bf16)
        out_refs[k][:, D:] = notes[CAP * k : CAP * (k + 1)].astype(bf16)


def forward_kernel(info_ref, base_ref, own_w_ref, other_w_ref, *refs):
    groups, (x_ref, keep_ref, part_ref, u_ref) = refs[:4], refs[-4:]
    grp, zh, y = info_ref[0], info_ref[1], info_ref[3]
    u_ref[:, :HID_DEV] = own_w_ref[:D, :]
    u_ref[:, HID_DEV:] = other_w_ref[:D, :]
    start = 0
    for ref in groups:
        count = ref.shape[0]
        x_ref[start : start + count, :] = ref[:, :D]
        keep_ref[start : start + count, 2 * HID_DEV :] = ref[:, D:].astype(f32)
        start += count
    pieces = jnp.concatenate([own_w_ref[D:, :], other_w_ref[D:, :]], axis=1).astype(f32)
    proj = pieces[0:1] + pieces[1:2] + pieces[2:3]
    pre = jnp.dot(x_ref[...], u_ref[...], preferred_element_type=f32)
    sig = jax.nn.sigmoid(pre)
    hidden = (pre * sig).astype(bf16)
    keep_ref[:ROWS, : 2 * HID_DEV] = pre
    keep_ref[ROWS:, : 2 * HID_DEV] = jnp.broadcast_to(proj, (8, 2 * HID_DEV))
    value = jnp.sum(hidden.astype(f32) * proj, axis=1, keepdims=True)
    lane = iota((CAP, 128), 1)
    token = iota((CAP, TOK_DEV), 1).astype(f32)
    row = iota((16, TOK_DEV), 0)
    total = jnp.where((row == zh * 4 + y) & (grp == 0), base_ref[0:1, :], 0.0)
    for at, k, d in BLOCKS:
        note = keep_ref[at : at + CAP, 2 * HID_DEV :]
        gate = jnp.sum(jnp.where((lane >= 1 + 3 * k) & (lane < 4 + 3 * k), note, 0.0), axis=1, keepdims=True)
        term = gate * value[at : at + CAP]
        spread = jnp.sum(jnp.where(note[:, 0:1] == token, term, 0.0), axis=0, keepdims=True)
        total = total + jnp.where(row == (zh ^ k) * 4 + (y ^ d), spread, 0.0)
    part_ref[...] = total


def backward_kernel(info_ref, table_ref, x_ref, keep_ref, own_ref, send_ref, own_head_ref):
    zh, c, y = info_ref[1], info_ref[4], info_ref[3]
    table = table_ref[...]
    note = keep_ref[:ROWS, 2 * HID_DEV :]
    token = iota((CAP, TOK_DEV), 1).astype(f32)
    lane = iota((CAP, 128), 1)
    mine, gates = [], []
    for at, k, d in BLOCKS:
        block = ((zh ^ k) * 4 + (y ^ d)) * 2 + c
        values = table_ref[pl.ds(block, 1), :]
        part = keep_ref[at : at + CAP, 2 * HID_DEV :]
        mine.append(jnp.sum(jnp.where(part[:, 0:1] == token, values, 0.0), axis=1, keepdims=True))
        gates.append(
            jnp.sum(jnp.where((lane >= 1 + 3 * k) & (lane < 4 + 3 * k), part, 0.0), axis=1, keepdims=True)
        )
    mine = jnp.concatenate(mine, axis=0)
    gate = jnp.concatenate(gates, axis=0)
    hot = jnp.where(iota((ROWS, 32), 1).astype(f32) == note[:, 13:14], 1.0, 0.0).astype(bf16)
    found = jnp.zeros((ROWS, TOK_DEV), f32)
    for part in thirds(table):
        found = found + jnp.dot(hot, part.astype(bf16), preferred_element_type=f32)
    places = iota((ROWS, TOK_DEV), 1).astype(f32)
    theirs = jnp.sum(jnp.where(places == note[:, 14:15], found, 0.0), axis=1, keepdims=True)
    side = note[:, 15:16]
    margin = side * (mine - theirs)
    grad = -side * (64.0 * jax.nn.sigmoid(-margin)) * gate
    pre = keep_ref[:ROWS, : 2 * HID_DEV]
    proj = keep_ref[ROWS : ROWS + 1, : 2 * HID_DEV]
    sig = jax.nn.sigmoid(pre)
    hidden = (pre * sig).astype(bf16).astype(f32)
    hid_grad = jnp.sum(grad * hidden, axis=0, keepdims=True)
    pre_grad = (grad * proj * (sig * (1.0 + pre * (1.0 - sig)))).astype(bf16)
    out = lax.dot_general(x_ref[...], pre_grad, (((0,), (0,)), ((), ())), preferred_element_type=f32)
    own_ref[...] = out[:, :HID_DEV]
    send_ref[:D, :] = out[:, HID_DEV:]
    own_head_ref[...] = jnp.broadcast_to(hid_grad[:, :HID_DEV], (8, HID_DEV))
    send_ref[D:, :] = jnp.broadcast_to(hid_grad[:, HID_DEV:], (8, HID_DEV))


def loss_kernel(table_ref, pair_ref, out_ref):
    parts = jnp.concatenate([p.astype(bf16) for p in thirds(table_ref[...])], axis=0)

    def rewards_of(index):
        high = jnp.floor(index * (1.0 / TOK_DEV))
        low = index - high * TOK_DEV
        count = index.shape[1]
        row = iota((96, count), 0) & 31
        hot = jnp.where(row.astype(f32) == high, 1.0, 0.0).astype(bf16)
        found = lax.dot_general(parts, hot, (((0,), (0,)), ((), ())), preferred_element_type=f32)
        return jnp.sum(jnp.where(iota((TOK_DEV, count), 0).astype(f32) == low, found, 0.0), axis=0, keepdims=True)

    def step(r, total):
        def line(at):
            rows = [pair_ref[pl.ds(at + i, 1), :].astype(f32) for i in range(4)]
            return jnp.concatenate(rows, axis=1)

        margin = rewards_of(line(4 * r)) - rewards_of(line(4 * r + 32))
        return total + jnp.maximum(-margin, 0.0) + jnp.log1p(jnp.exp(-jnp.abs(margin)))

    total = lax.fori_loop(0, 8, step, jnp.zeros((1, 512), f32))
    out_ref[...] = jnp.broadcast_to(jnp.sum(total, axis=1, keepdims=True) * (1.0 / PAIRS), (1, 128))


def final_kernel(
    take_ref, up_ref, up_got_ref, down_ref, down_got_ref, own_ref, recv_ref, own_head_ref, head_ref, new_up_ref, new_down_ref
):
    step = own_ref[...] + recv_ref[:D, :]
    grad = own_head_ref[0:1] + recv_ref[D : D + 1, :]
    square = (HID_DEV, HID_DEV)
    column = jnp.sum(jnp.where(iota(square, 0) == iota(square, 1), grad, 0.0), axis=1, keepdims=True)
    head = head_ref[...].astype(f32)
    for wanted, ref in ((1, up_got_ref), (0, up_ref)):

        @pl.when(take_ref[0] == wanted)
        def _(ref=ref):
            new_up_ref[...] = (ref[...].astype(f32) + step).astype(bf16)

    for wanted, ref in ((1, down_got_ref), (0, down_ref)):

        @pl.when(take_ref[1] == wanted)
        def _(ref=ref):
            for j in range(D // HID_DEV):
                at = j * HID_DEV
                old = ref[at : at + HID_DEV, :].astype(f32)
                new_down_ref[:, at : at + HID_DEV] = (old + column * head[j : j + 1]).astype(bf16)


def pick_kernel(count, take_ref, *refs):
    got_refs, own_refs, out_refs = refs[:count], refs[count : 2 * count], refs[-count:]
    for i in range(count):

        @pl.when(take_ref[i] == 1)
        def _(i=i):
            out_refs[i][...] = got_refs[i][...]

        @pl.when(take_ref[i] == 0)
        def _(i=i):
            out_refs[i][...] = own_refs[i][...]


def split_kernel(take_ref, got_ref, own_ref, earlier_ref, up_ref, down_ref):
    for wanted, ref in ((1, got_ref), (0, own_ref)):

        @pl.when(take_ref[0] == wanted)
        def _(ref=ref):
            up_ref[...] = ref[:D, :]
            down_ref[...] = ref[D:, :]


def join_kernel(*refs):
    for k in range(EXP_GRP):
        refs[-1][CAP * k : CAP * (k + 1), :] = refs[k][...]


def swap(block, axis, mask):
    count = lax.axis_size(axis)
    return lax.ppermute(block, axis, [(i, i ^ mask) for i in range(count)])


def picks(stages, got, own, *earlier):
    count = len(stages)
    return pl.pallas_call(
        functools.partial(pick_kernel, count),
        out_shape=[shape(o.shape, o.dtype) for o in own],
        in_specs=[SMEM] + [VMEM] * (2 * count) + [ANY] * len(earlier),
        out_specs=[VMEM] * count,
        compiler_params=PARAMS,
        cost_estimate=SPACED,
        name="pick",
    )(jnp.concatenate([s[2] for s in stages]), *got, *own, *earlier)


def pick(stage, got, own, *earlier):
    return picks([stage], [got], [own], *earlier)[0]


def join(blocks, *earlier):
    return pl.pallas_call(
        join_kernel,
        out_shape=shape((EXP_GRP * CAP, WIDE), bf16),
        in_specs=[VMEM] * EXP_GRP + [ANY] * len(earlier),
        out_specs=VMEM,
        compiler_params=PARAMS,
        cost_estimate=SPACED,
        name="join",
    )(*blocks, *earlier)


def body(tokens, routes, gate_values, old_group, move_mask, pair_index, reward_head, w_up, w_down, acc_up, acc_down):
    x, zl, zh, y, c = (lax.axis_index(a) for a in ("x", "zl", "zh", "y", "c"))
    info = jnp.stack([x * 4 + zl, zh, zh * 8 + y * 2 + c, y, c]).astype(jnp.int32)
    head = reward_head.reshape(D // 128, 128)
    pairs = pair_index.reshape(64, 128)
    mask = jnp.sum(jnp.where(jnp.arange(EXP_GRP) == zh, move_mask, 0))
    bit = [jnp.bitwise_and(jnp.right_shift(mask, i), 1) for i in range(4)]
    x1 = ("x", 1, jnp.bitwise_xor(bit[2], bit[3]).reshape(1))
    x3 = ("x", 3, bit[3].reshape(1))
    z1 = ("zl", 1, bit[0].reshape(1))
    z2 = ("zl", 2, bit[1].reshape(1))

    *sent, base, weights, accums = pl.pallas_call(
        dispatch_kernel,
        out_shape=[shape((CAP, WIDE), bf16)] * 4 + [shape((8, TOK_DEV), f32), shape((D + 16, HID_DEV), bf16), shape((2 * D, HID_DEV), bf16)],
        in_specs=[SMEM] * 3 + [VMEM] * 9,
        out_specs=[VMEM] * 7,
        compiler_params=pltpu.CompilerParams(vmem_limit_bytes=63 * 1024 * 1024),
        name="dispatch",
    )(
        old_group,
        move_mask,
        info,
        tokens,
        routes.T,
        gate_values.T,
        pairs,
        head,
        w_up[0],
        w_down[0],
        acc_up[0],
        acc_down[0],
    )
    blocks = [sent[0], swap(sent[1], "zh", 1), swap(sent[2], "zh", 2), swap(sent[3], "zh", 3)]
    got = swap(weights, *x1[:2])
    acc_got = swap(accums, *x1[:2])
    weights = pick(x1, got, weights)
    got = swap(weights, *x3[:2])
    accums = pick(x1, acc_got, accums, weights)
    acc_got = swap(accums, *x3[:2])
    weights = pick(x3, got, weights, accums)
    got = swap(weights, *z1[:2])
    rows = join(blocks, weights)
    held = [rows] + [swap(rows, "y", d) for d in (1, 2, 3)]
    weights = pick(z1, got, weights, rows)
    got = swap(weights, *z2[:2])
    up, down = pl.pallas_call(
        split_kernel,
        out_shape=[shape((D, HID_DEV), bf16)] * 2,
        in_specs=[SMEM, VMEM, VMEM, ANY],
        out_specs=[VMEM] * 2,
        compiler_params=PARAMS,
        cost_estimate=SPACED,
        name="pick_split",
    )(x3[2], acc_got, accums, weights)
    weights = pick(z2, got, weights, up)
    weights, up, down = lax.optimization_barrier((weights, up, down))
    other_weights = swap(weights, "c", 1)
    up_got = swap(up, *z1[:2])
    down_got = swap(down, *z2[:2])

    xs, keep, part = pl.pallas_call(
        forward_kernel,
        out_shape=[
            shape((ROWS, D), bf16),
            shape((ROWS + 8, 2 * HID_DEV + 128), f32),
            shape((16, TOK_DEV), f32),
        ],
        in_specs=[SMEM] + [VMEM] * 7,
        out_specs=[VMEM] * 3,
        scratch_shapes=[pltpu.VMEM((D, 2 * HID_DEV), bf16)],
        compiler_params=PARAMS,
        name="forward",
    )(info, base, weights, other_weights, *held)

    mine = lax.all_to_all(part, ("x", "y"), 0, 0, tiled=True)
    mine = jnp.broadcast_to(jnp.sum(mine, axis=0, keepdims=True), (16, TOK_DEV))
    mine = lax.all_to_all(mine, ("zl", "zh"), 0, 0, tiled=True)
    mine = jnp.broadcast_to(jnp.sum(mine, axis=0, keepdims=True), (32, TOK_DEV))
    up, down = picks([z1, z2], [up_got, down_got], [up, down], mine)
    mine, up, down = lax.optimization_barrier((mine, up, down))
    up_got = swap(up, *z2[:2])
    down_got = swap(down, *z1[:2])
    table = lax.all_to_all(mine, ("x", "y", "c"), 0, 0, tiled=True)

    own, send, own_head = pl.pallas_call(
        backward_kernel,
        out_shape=[shape((D, HID_DEV), f32), shape((D + 8, HID_DEV), f32), shape((8, HID_DEV), f32)],
        in_specs=[SMEM] + [VMEM] * 3,
        out_specs=[VMEM] * 3,
        compiler_params=PARAMS,
        cost_estimate=SPACED,
        name="backward",
    )(info, table, xs, keep)
    recv = swap(send, "c", 1)
    loss = pl.pallas_call(
        loss_kernel,
        out_shape=shape((1, 128), f32),
        in_specs=[VMEM] * 2,
        out_specs=VMEM,
        compiler_params=PARAMS,
        cost_estimate=SPACED,
        name="loss",
    )(table, pairs)
    new_up, new_down = pl.pallas_call(
        final_kernel,
        out_shape=[shape((D, HID_DEV), bf16), shape((HID_DEV, D), bf16)],
        in_specs=[SMEM] + [VMEM] * 8,
        out_specs=[VMEM] * 2,
        compiler_params=PARAMS,
        name="final",
    )(jnp.concatenate([z2[2], z1[2]]), up, up_got, down, down_got, own, recv, own_head, head)
    return new_up[None], new_down[None], loss[0, 0]


def solution(mesh):
    fine = Mesh(mesh.devices.reshape(4, 4, 4, 4, 2), ("x", "zl", "zh", "y", "c"))
    grp, ep = ("x", "zl"), ("zh", "y", "c")
    return jax.shard_map(
        body,
        mesh=fine,
        in_specs=(P(ep, None), P(ep, None), P(ep, None), P(), P(), P(), P())
        + (P(grp, None, ep), P(grp, ep, None)) * 2,
        out_specs=(P(grp, None, ep), P(grp, ep, None), P()),
        check_vma=False,
    )
```

```python
import functools

import jax
import jax.numpy as jnp
from jax import lax
from jax.experimental import pallas as pl
from jax.experimental.pallas import tpu as pltpu
from jax.sharding import Mesh
from jax.sharding import PartitionSpec as P

D = 2048
HID_DEV = 128
EXP_GRP = 4
TOK_DEV = 256
CAP = 48
WIDE = D + 128
ROWS = 16 * CAP
PAIRS = 4096

f32 = jnp.float32
bf16 = jnp.bfloat16
VMEM = pl.BlockSpec(memory_space=pltpu.VMEM)
SMEM = pl.BlockSpec(memory_space=pltpu.SMEM)
PARAMS = pltpu.CompilerParams(vmem_limit_bytes=24 * 1024 * 1024)
NT = (((1,), (1,)), ((), ()))

BLOCKS = [(CAP * d, 0, d) for d in range(4)] + [
    (4 * CAP + 3 * CAP * d + CAP * (k - 1), k, d) for d in range(4) for k in range(1, EXP_GRP)
]
SPACED = pl.CostEstimate(flops=10**11, bytes_accessed=0, transcendentals=0)
ANY = pl.BlockSpec(memory_space=pl.ANY)


def shape(dims, kind):
    return jax.ShapeDtypeStruct(dims, kind)


def iota(dims, axis):
    return lax.broadcasted_iota(jnp.int32, dims, axis)


def thirds(value):
    first = value.astype(bf16).astype(f32)
    second = (value - first).astype(bf16).astype(f32)
    third = (value - first - second).astype(bf16).astype(f32)
    return first, second, third


def dispatch_kernel(
    group_ref,
    mask_ref,
    info_ref,
    tok_ref,
    routes_ref,
    gates_ref,
    pair_ref,
    head_ref,
    up_ref,
    down_ref,
    acc_up_ref,
    acc_down_ref,
    *outs,
):
    out_ref, own_ref, base_ref, weights_ref, acc_ref = outs
    acc_ref[:D, :] = acc_up_ref[...]
    for j in range(D // HID_DEV):
        at = j * HID_DEV
        acc_ref[D + at : D + at + HID_DEV, :] = acc_down_ref[:, at : at + HID_DEV]
    weights_ref[:D, :] = up_ref[...]
    head = head_ref[...].astype(f32)
    head = jnp.concatenate([head[j : j + 1] for j in range(D // 128)], axis=1)
    head = jnp.broadcast_to(head, (16, D)).astype(bf16)
    proj = lax.dot_general(head, down_ref[...], NT, preferred_element_type=f32)
    first, second, third = thirds(proj)
    row = iota((16, HID_DEV), 0)
    packed = jnp.where(row == 0, first, jnp.where(row == 1, second, jnp.where(row == 2, third, 0.0)))
    weights_ref[D:, :] = packed.astype(bf16)
    grp, zh, member = info_ref[0], info_ref[1], info_ref[2]
    routes = routes_ref[...]
    gates = gates_ref[...]
    sel, gate = [], []
    for k in range(EXP_GRP):
        slot = k
        mask = mask_ref[slot]
        expert = jnp.int32(0)
        for j in range(16):
            found = (group_ref[4 * j + slot] ^ mask) == grp
            expert = jnp.where(found, 4 * j + slot, expert)
        hit = routes == expert
        sel.append(jnp.sum(jnp.where(hit, 1.0, 0.0), axis=0, keepdims=True))
        gate.append(jnp.sum(jnp.where(hit, gates, 0.0), axis=0, keepdims=True))
    row8 = iota((8, TOK_DEV), 0)
    chosen = jnp.zeros((8, TOK_DEV), f32)
    for k in range(EXP_GRP):
        chosen = jnp.where(row8 == k, sel[k], chosen)
    tri = jnp.where(iota((TOK_DEV, TOK_DEV), 0) <= iota((TOK_DEV, TOK_DEV), 1), 1.0, 0.0).astype(bf16)
    place = jnp.dot(chosen.astype(bf16), tri, preferred_element_type=f32) - 1.0
    own = (iota((TOK_DEV, 1), 0) + member * TOK_DEV).astype(f32)

    def look(r, code):
        first = pair_ref[pl.ds(r, 1), :].astype(f32)
        second = pair_ref[pl.ds(r + 32, 1), :].astype(f32)
        return jnp.where(first == own, second + 1.0, jnp.where(second == own, -1.0 - first, code))

    code = lax.fori_loop(0, 32, look, jnp.zeros((TOK_DEV, 128), f32), unroll=4)
    code = jnp.sum(code, axis=1, keepdims=True)
    partner = jnp.abs(code) - 1.0
    high = jnp.floor(partner * (1.0 / TOK_DEV))
    low = partner - high * TOK_DEV
    lane = iota((TOK_DEV, 128), 1)
    by_token = jnp.where(lane == 13, high, jnp.where(lane == 14, low, jnp.where(lane == 15, jnp.where(code > 0, 1.0, -1.0), 0.0)))
    by_token = jnp.where(lane == 0, iota((TOK_DEV, 128), 0).astype(f32), by_token).astype(bf16)
    rows = iota((128, TOK_DEV), 0)
    by_slot = jnp.zeros((128, TOK_DEV), f32)
    for k in range(EXP_GRP):
        for j, part in enumerate(thirds(gate[k])):
            by_slot = jnp.where(rows == 1 + 3 * k + j, part, by_slot)
    by_slot = by_slot.astype(bf16)
    base_ref[...] = lax.dot_general(head, tok_ref[...], NT, preferred_element_type=f32)[:8]
    height = iota((CAP, TOK_DEV), 0).astype(f32)
    picks = [
        jnp.where((place[k : k + 1] == height) & (sel[k] > 0.5), 1.0, 0.0).astype(bf16) for k in range(EXP_GRP)
    ]
    pick = jnp.concatenate(picks, axis=0)
    notes = jnp.dot(pick, by_token, preferred_element_type=f32) + lax.dot_general(
        pick, by_slot, NT, preferred_element_type=f32
    )
    wide = jnp.dot(pick, tok_ref[...], preferred_element_type=f32)
    out_ref[:, :D] = wide.astype(bf16)
    out_ref[:, D:] = notes.astype(bf16)
    own_ref[...] = out_ref[pl.ds(pl.multiple_of(zh * CAP, CAP), CAP), :]


def forward_kernel(info_ref, base_ref, own_w_ref, other_w_ref, *refs):
    groups, (x_ref, keep_ref, part_ref, u_ref) = refs[:8], refs[8:]
    grp, zh, y = info_ref[0], info_ref[1], info_ref[3]
    u_ref[:, :HID_DEV] = own_w_ref[:D, :]
    u_ref[:, HID_DEV:] = other_w_ref[:D, :]
    start = 0
    for ref in groups:
        count = ref.shape[0]
        x_ref[start : start + count, :] = ref[:, :D]
        keep_ref[start : start + count, 2 * HID_DEV :] = ref[:, D:].astype(f32)
        start += count
    pieces = jnp.concatenate([own_w_ref[D:, :], other_w_ref[D:, :]], axis=1).astype(f32)
    proj = pieces[0:1] + pieces[1:2] + pieces[2:3]
    pre = jnp.dot(x_ref[...], u_ref[...], preferred_element_type=f32)
    sig = jax.nn.sigmoid(pre)
    hidden = (pre * sig).astype(bf16)
    keep_ref[:ROWS, : 2 * HID_DEV] = pre
    keep_ref[ROWS:, : 2 * HID_DEV] = jnp.broadcast_to(proj, (8, 2 * HID_DEV))
    value = jnp.sum(hidden.astype(f32) * proj, axis=1, keepdims=True)
    lane = iota((CAP, 128), 1)
    token = iota((CAP, TOK_DEV), 1).astype(f32)
    row = iota((16, TOK_DEV), 0)
    total = jnp.where((row == zh * 4 + y) & (grp == 0), base_ref[0:1, :], 0.0)
    for at, k, d in BLOCKS:
        note = keep_ref[at : at + CAP, 2 * HID_DEV :]
        gate = jnp.sum(jnp.where((lane >= 1 + 3 * zh) & (lane < 4 + 3 * zh), note, 0.0), axis=1, keepdims=True)
        term = gate * value[at : at + CAP]
        spread = jnp.sum(jnp.where(note[:, 0:1] == token, term, 0.0), axis=0, keepdims=True)
        total = total + jnp.where(row == (zh ^ k) * 4 + (y ^ d), spread, 0.0)
    part_ref[...] = total


def backward_kernel(info_ref, table_ref, x_ref, keep_ref, own_ref, send_ref, own_head_ref):
    zh, c, y = info_ref[1], info_ref[4], info_ref[3]
    table = table_ref[...]
    note = keep_ref[:ROWS, 2 * HID_DEV :]
    token = iota((CAP, TOK_DEV), 1).astype(f32)
    lane = iota((CAP, 128), 1)
    mine, gates = [], []
    for at, k, d in BLOCKS:
        block = ((zh ^ k) * 4 + (y ^ d)) * 2 + c
        values = table_ref[pl.ds(block, 1), :]
        part = keep_ref[at : at + CAP, 2 * HID_DEV :]
        mine.append(jnp.sum(jnp.where(part[:, 0:1] == token, values, 0.0), axis=1, keepdims=True))
        gates.append(
            jnp.sum(jnp.where((lane >= 1 + 3 * zh) & (lane < 4 + 3 * zh), part, 0.0), axis=1, keepdims=True)
        )
    mine = jnp.concatenate(mine, axis=0)
    gate = jnp.concatenate(gates, axis=0)
    hot = jnp.where(iota((ROWS, 32), 1).astype(f32) == note[:, 13:14], 1.0, 0.0).astype(bf16)
    found = jnp.zeros((ROWS, TOK_DEV), f32)
    for part in thirds(table):
        found = found + jnp.dot(hot, part.astype(bf16), preferred_element_type=f32)
    places = iota((ROWS, TOK_DEV), 1).astype(f32)
    theirs = jnp.sum(jnp.where(places == note[:, 14:15], found, 0.0), axis=1, keepdims=True)
    side = note[:, 15:16]
    margin = side * (mine - theirs)
    grad = -side * (64.0 * jax.nn.sigmoid(-margin)) * gate
    pre = keep_ref[:ROWS, : 2 * HID_DEV]
    proj = keep_ref[ROWS : ROWS + 1, : 2 * HID_DEV]
    sig = jax.nn.sigmoid(pre)
    hidden = (pre * sig).astype(bf16).astype(f32)
    hid_grad = jnp.sum(grad * hidden, axis=0, keepdims=True)
    pre_grad = (grad * proj * (sig * (1.0 + pre * (1.0 - sig)))).astype(bf16)
    out = lax.dot_general(x_ref[...], pre_grad, (((0,), (0,)), ((), ())), preferred_element_type=f32)
    own_ref[...] = out[:, :HID_DEV]
    send_ref[:D, :] = out[:, HID_DEV:]
    own_head_ref[...] = jnp.broadcast_to(hid_grad[:, :HID_DEV], (8, HID_DEV))
    send_ref[D:, :] = jnp.broadcast_to(hid_grad[:, HID_DEV:], (8, HID_DEV))


def loss_kernel(table_ref, pair_ref, out_ref):
    parts = jnp.concatenate([p.astype(bf16) for p in thirds(table_ref[...])], axis=0)

    def rewards_of(index):
        high = jnp.floor(index * (1.0 / TOK_DEV))
        low = index - high * TOK_DEV
        count = index.shape[1]
        row = iota((96, count), 0) & 31
        hot = jnp.where(row.astype(f32) == high, 1.0, 0.0).astype(bf16)
        found = lax.dot_general(parts, hot, (((0,), (0,)), ((), ())), preferred_element_type=f32)
        return jnp.sum(jnp.where(iota((TOK_DEV, count), 0).astype(f32) == low, found, 0.0), axis=0, keepdims=True)

    def step(r, total):
        def line(at):
            rows = [pair_ref[pl.ds(at + i, 1), :].astype(f32) for i in range(4)]
            return jnp.concatenate(rows, axis=1)

        margin = rewards_of(line(4 * r)) - rewards_of(line(4 * r + 32))
        return total + jnp.maximum(-margin, 0.0) + jnp.log1p(jnp.exp(-jnp.abs(margin)))

    total = lax.fori_loop(0, 8, step, jnp.zeros((1, 512), f32))
    out_ref[...] = jnp.broadcast_to(jnp.sum(total, axis=1, keepdims=True) * (1.0 / PAIRS), (1, 128))


def final_kernel(
    take_ref, up_ref, up_got_ref, down_ref, down_got_ref, own_ref, recv_ref, own_head_ref, head_ref, new_up_ref, new_down_ref
):
    step = own_ref[...] + recv_ref[:D, :]
    grad = own_head_ref[0:1] + recv_ref[D : D + 1, :]
    square = (HID_DEV, HID_DEV)
    column = jnp.sum(jnp.where(iota(square, 0) == iota(square, 1), grad, 0.0), axis=1, keepdims=True)
    head = head_ref[...].astype(f32)
    for wanted, ref in ((1, up_got_ref), (0, up_ref)):

        @pl.when(take_ref[0] == wanted)
        def _(ref=ref):
            new_up_ref[...] = (ref[...].astype(f32) + step).astype(bf16)

    for wanted, ref in ((1, down_got_ref), (0, down_ref)):

        @pl.when(take_ref[1] == wanted)
        def _(ref=ref):
            for j in range(D // HID_DEV):
                at = j * HID_DEV
                old = ref[at : at + HID_DEV, :].astype(f32)
                new_down_ref[:, at : at + HID_DEV] = (old + column * head[j : j + 1]).astype(bf16)


def pick_kernel(count, take_ref, *refs):
    got_refs, own_refs, out_refs = refs[:count], refs[count : 2 * count], refs[-count:]
    for i in range(count):

        @pl.when(take_ref[i] == 1)
        def _(i=i):
            out_refs[i][...] = got_refs[i][...]

        @pl.when(take_ref[i] == 0)
        def _(i=i):
            out_refs[i][...] = own_refs[i][...]


def split_kernel(take_ref, got_ref, own_ref, earlier_ref, up_ref, down_ref):
    for wanted, ref in ((1, got_ref), (0, own_ref)):

        @pl.when(take_ref[0] == wanted)
        def _(ref=ref):
            up_ref[...] = ref[:D, :]
            down_ref[...] = ref[D:, :]


def others_kernel(info_ref, rows_ref, *refs):
    zh = info_ref[1]
    for k in range(1, EXP_GRP):
        block = rows_ref[pl.ds(pl.multiple_of((zh ^ k) * CAP, CAP), CAP), :]
        refs[-1][CAP * (k - 1) : CAP * k, :] = block


def swap(block, axis, mask):
    count = lax.axis_size(axis)
    return lax.ppermute(block, axis, [(i, i ^ mask) for i in range(count)])


def picks(stages, got, own, *earlier):
    count = len(stages)
    return pl.pallas_call(
        functools.partial(pick_kernel, count),
        out_shape=[shape(o.shape, o.dtype) for o in own],
        in_specs=[SMEM] + [VMEM] * (2 * count) + [ANY] * len(earlier),
        out_specs=[VMEM] * count,
        compiler_params=PARAMS,
        cost_estimate=SPACED,
        name="pick",
    )(jnp.concatenate([s[2] for s in stages]), *got, *own, *earlier)


def pick(stage, got, own, *earlier):
    return picks([stage], [got], [own], *earlier)[0]


def others(info, rows, *earlier):
    return pl.pallas_call(
        others_kernel,
        out_shape=shape((3 * CAP, WIDE), bf16),
        in_specs=[SMEM, VMEM] + [ANY] * len(earlier),
        out_specs=VMEM,
        compiler_params=PARAMS,
        cost_estimate=SPACED,
        name="others",
    )(info, rows, *earlier)


def body(tokens, routes, gate_values, old_group, move_mask, pair_index, reward_head, w_up, w_down, acc_up, acc_down):
    x, zl, zh, y, c = (lax.axis_index(a) for a in ("x", "zl", "zh", "y", "c"))
    info = jnp.stack([x * 4 + zl, zh, zh * 8 + y * 2 + c, y, c]).astype(jnp.int32)
    head = reward_head.reshape(D // 128, 128)
    pairs = pair_index.reshape(64, 128)
    mask = jnp.sum(jnp.where(jnp.arange(EXP_GRP) == zh, move_mask, 0))
    bit = [jnp.bitwise_and(jnp.right_shift(mask, i), 1) for i in range(4)]
    x1 = ("x", 1, jnp.bitwise_xor(bit[2], bit[3]).reshape(1))
    x3 = ("x", 3, bit[3].reshape(1))
    z1 = ("zl", 1, bit[0].reshape(1))
    z2 = ("zl", 2, bit[1].reshape(1))

    sent, own_rows, base, weights, accums = pl.pallas_call(
        dispatch_kernel,
        out_shape=[
            shape((EXP_GRP * CAP, WIDE), bf16),
            shape((CAP, WIDE), bf16),
            shape((8, TOK_DEV), f32),
            shape((D + 16, HID_DEV), bf16),
            shape((2 * D, HID_DEV), bf16),
        ],
        in_specs=[SMEM] * 3 + [VMEM] * 9,
        out_specs=[VMEM] * 5,
        compiler_params=pltpu.CompilerParams(vmem_limit_bytes=63 * 1024 * 1024),
        name="dispatch",
    )(
        old_group,
        move_mask,
        info,
        tokens,
        routes.T,
        gate_values.T,
        pairs,
        head,
        w_up[0],
        w_down[0],
        acc_up[0],
        acc_down[0],
    )
    arrived = lax.all_to_all(sent, "zh", 0, 0, tiled=True)
    held = [own_rows] + [swap(own_rows, "y", d) for d in (1, 2, 3)]
    got = swap(weights, *x1[:2])
    acc_got = swap(accums, *x1[:2])
    weights = pick(x1, got, weights)
    got = swap(weights, *x3[:2])
    accums = pick(x1, acc_got, accums, weights)
    acc_got = swap(accums, *x3[:2])
    weights = pick(x3, got, weights, accums)
    got = swap(weights, *z1[:2])
    rows = others(info, arrived, weights, *held[1:])
    held += [rows] + [swap(rows, "y", d) for d in (1, 2, 3)]
    weights = pick(z1, got, weights, rows)
    got = swap(weights, *z2[:2])
    up, down = pl.pallas_call(
        split_kernel,
        out_shape=[shape((D, HID_DEV), bf16)] * 2,
        in_specs=[SMEM, VMEM, VMEM, ANY],
        out_specs=[VMEM] * 2,
        compiler_params=PARAMS,
        cost_estimate=SPACED,
        name="pick_split",
    )(x3[2], acc_got, accums, weights)
    weights = pick(z2, got, weights, up)
    weights, up, down = lax.optimization_barrier((weights, up, down))
    other_weights = swap(weights, "c", 1)
    up_got = swap(up, *z1[:2])
    down_got = swap(down, *z2[:2])

    xs, keep, part = pl.pallas_call(
        forward_kernel,
        out_shape=[
            shape((ROWS, D), bf16),
            shape((ROWS + 8, 2 * HID_DEV + 128), f32),
            shape((16, TOK_DEV), f32),
        ],
        in_specs=[SMEM] + [VMEM] * 11,
        out_specs=[VMEM] * 3,
        scratch_shapes=[pltpu.VMEM((D, 2 * HID_DEV), bf16)],
        compiler_params=PARAMS,
        name="forward",
    )(info, base, weights, other_weights, *held)

    mine = lax.all_to_all(part, ("x", "y"), 0, 0, tiled=True)
    mine = jnp.broadcast_to(jnp.sum(mine, axis=0, keepdims=True), (16, TOK_DEV))
    mine = lax.all_to_all(mine, ("zl", "zh"), 0, 0, tiled=True)
    mine = jnp.broadcast_to(jnp.sum(mine, axis=0, keepdims=True), (32, TOK_DEV))
    up, down = picks([z1, z2], [up_got, down_got], [up, down], mine)
    mine, up, down = lax.optimization_barrier((mine, up, down))
    up_got = swap(up, *z2[:2])
    down_got = swap(down, *z1[:2])
    table = lax.all_to_all(mine, ("x", "y", "c"), 0, 0, tiled=True)

    own, send, own_head = pl.pallas_call(
        backward_kernel,
        out_shape=[shape((D, HID_DEV), f32), shape((D + 8, HID_DEV), f32), shape((8, HID_DEV), f32)],
        in_specs=[SMEM] + [VMEM] * 3,
        out_specs=[VMEM] * 3,
        compiler_params=PARAMS,
        cost_estimate=SPACED,
        name="backward",
    )(info, table, xs, keep)
    recv = swap(send, "c", 1)
    loss = pl.pallas_call(
        loss_kernel,
        out_shape=shape((1, 128), f32),
        in_specs=[VMEM] * 2,
        out_specs=VMEM,
        compiler_params=PARAMS,
        cost_estimate=SPACED,
        name="loss",
    )(table, pairs)
    new_up, new_down = pl.pallas_call(
        final_kernel,
        out_shape=[shape((D, HID_DEV), bf16), shape((HID_DEV, D), bf16)],
        in_specs=[SMEM] + [VMEM] * 8,
        out_specs=[VMEM] * 2,
        compiler_params=PARAMS,
        name="final",
    )(jnp.concatenate([z2[2], z1[2]]), up, up_got, down, down_got, own, recv, own_head, head)
    return new_up[None], new_down[None], loss[0, 0]


def solution(mesh):
    fine = Mesh(mesh.devices.reshape(4, 4, 4, 4, 2), ("x", "zl", "zh", "y", "c"))
    grp, ep = ("x", "zl"), ("zh", "y", "c")
    return jax.shard_map(
        body,
        mesh=fine,
        in_specs=(P(ep, None), P(ep, None), P(ep, None), P(), P(), P(), P())
        + (P(grp, None, ep), P(grp, ep, None)) * 2,
        out_specs=(P(grp, None, ep), P(grp, ep, None), P()),
        check_vma=False,
    )
```

```python
import functools

import jax
import jax.numpy as jnp
from jax import lax
from jax.experimental import pallas as pl
from jax.experimental.pallas import tpu as pltpu
from jax.sharding import Mesh
from jax.sharding import PartitionSpec as P

D = 2048
HID_DEV = 128
EXP_GRP = 4
TOK_DEV = 256
CAP = 48
WIDE = D + 128
ROWS = 16 * CAP
PAIRS = 4096

f32 = jnp.float32
bf16 = jnp.bfloat16
VMEM = pl.BlockSpec(memory_space=pltpu.VMEM)
SMEM = pl.BlockSpec(memory_space=pltpu.SMEM)
PARAMS = pltpu.CompilerParams(vmem_limit_bytes=24 * 1024 * 1024)
NT = (((1,), (1,)), ((), ()))

BLOCKS = [(CAP * d, 0, d) for d in range(4)] + [
    (4 * CAP + 3 * CAP * d + CAP * (k - 1), k, d) for d in range(4) for k in range(1, EXP_GRP)
]
LIGHT = pl.CostEstimate(flops=0, bytes_accessed=0, transcendentals=0)
SPACED = pl.CostEstimate(flops=10**11, bytes_accessed=0, transcendentals=0)
ANY = pl.BlockSpec(memory_space=pl.ANY)


def shape(dims, kind):
    return jax.ShapeDtypeStruct(dims, kind)


def iota(dims, axis):
    return lax.broadcasted_iota(jnp.int32, dims, axis)


def thirds(value):
    first = value.astype(bf16).astype(f32)
    second = (value - first).astype(bf16).astype(f32)
    third = (value - first - second).astype(bf16).astype(f32)
    return first, second, third


def dispatch_kernel(
    group_ref,
    mask_ref,
    info_ref,
    tok_ref,
    routes_ref,
    gates_ref,
    pair_ref,
    head_ref,
    up_ref,
    down_ref,
    acc_up_ref,
    acc_down_ref,
    *outs,
):
    out_ref, own_ref, base_ref, weights_ref, acc_ref = outs
    acc_ref[:D, :] = acc_up_ref[...]
    for j in range(D // HID_DEV):
        at = j * HID_DEV
        acc_ref[D + at : D + at + HID_DEV, :] = acc_down_ref[:, at : at + HID_DEV]
    weights_ref[:D, :] = up_ref[...]
    head = head_ref[...].astype(f32)
    head = jnp.concatenate([head[j : j + 1] for j in range(D // 128)], axis=1)
    head = jnp.broadcast_to(head, (16, D)).astype(bf16)
    proj = lax.dot_general(head, down_ref[...], NT, preferred_element_type=f32)
    first, second, third = thirds(proj)
    row = iota((16, HID_DEV), 0)
    packed = jnp.where(row == 0, first, jnp.where(row == 1, second, jnp.where(row == 2, third, 0.0)))
    weights_ref[D:, :] = packed.astype(bf16)
    grp, zh, member = info_ref[0], info_ref[1], info_ref[2]
    routes = routes_ref[...]
    gates = gates_ref[...]
    sel, gate = [], []
    for k in range(EXP_GRP):
        slot = k
        mask = mask_ref[slot]
        expert = jnp.int32(0)
        for j in range(16):
            found = (group_ref[4 * j + slot] ^ mask) == grp
            expert = jnp.where(found, 4 * j + slot, expert)
        hit = routes == expert
        sel.append(jnp.sum(jnp.where(hit, 1.0, 0.0), axis=0, keepdims=True))
        gate.append(jnp.sum(jnp.where(hit, gates, 0.0), axis=0, keepdims=True))
    row8 = iota((8, TOK_DEV), 0)
    chosen = jnp.zeros((8, TOK_DEV), f32)
    for k in range(EXP_GRP):
        chosen = jnp.where(row8 == k, sel[k], chosen)
    tri = jnp.where(iota((TOK_DEV, TOK_DEV), 0) <= iota((TOK_DEV, TOK_DEV), 1), 1.0, 0.0).astype(bf16)
    place = jnp.dot(chosen.astype(bf16), tri, preferred_element_type=f32) - 1.0
    own = (iota((TOK_DEV, 1), 0) + member * TOK_DEV).astype(f32)

    def look(r, code):
        first = pair_ref[pl.ds(r, 1), :].astype(f32)
        second = pair_ref[pl.ds(r + 32, 1), :].astype(f32)
        return jnp.where(first == own, second + 1.0, jnp.where(second == own, -1.0 - first, code))

    code = lax.fori_loop(0, 32, look, jnp.zeros((TOK_DEV, 128), f32), unroll=4)
    code = jnp.sum(code, axis=1, keepdims=True)
    partner = jnp.abs(code) - 1.0
    high = jnp.floor(partner * (1.0 / TOK_DEV))
    low = partner - high * TOK_DEV
    lane = iota((TOK_DEV, 128), 1)
    by_token = jnp.where(lane == 13, high, jnp.where(lane == 14, low, jnp.where(lane == 15, jnp.where(code > 0, 1.0, -1.0), 0.0)))
    by_token = jnp.where(lane == 0, iota((TOK_DEV, 128), 0).astype(f32), by_token).astype(bf16)
    rows = iota((128, TOK_DEV), 0)
    by_slot = jnp.zeros((128, TOK_DEV), f32)
    for k in range(EXP_GRP):
        for j, part in enumerate(thirds(gate[k])):
            by_slot = jnp.where(rows == 1 + 3 * k + j, part, by_slot)
    by_slot = by_slot.astype(bf16)
    base_ref[...] = lax.dot_general(head, tok_ref[...], NT, preferred_element_type=f32)[:8]
    height = iota((CAP, TOK_DEV), 0).astype(f32)
    picks = [
        jnp.where((place[k : k + 1] == height) & (sel[k] > 0.5), 1.0, 0.0).astype(bf16) for k in range(EXP_GRP)
    ]
    pick = jnp.concatenate(picks, axis=0)
    notes = jnp.dot(pick, by_token, preferred_element_type=f32) + lax.dot_general(
        pick, by_slot, NT, preferred_element_type=f32
    )
    wide = jnp.dot(pick, tok_ref[...], preferred_element_type=f32)
    out_ref[:, :D] = wide.astype(bf16)
    out_ref[:, D:] = notes.astype(bf16)
    own_ref[...] = out_ref[pl.ds(pl.multiple_of(zh * CAP, CAP), CAP), :]


def forward_kernel(info_ref, base_ref, own_w_ref, other_w_ref, *refs):
    groups, (x_ref, keep_ref, part_ref, u_ref) = refs[:8], refs[8:]
    grp, zh, y = info_ref[0], info_ref[1], info_ref[3]
    u_ref[:, :HID_DEV] = own_w_ref[:D, :]
    u_ref[:, HID_DEV:] = other_w_ref[:D, :]
    start = 0
    for ref in groups:
        count = ref.shape[0]
        x_ref[start : start + count, :] = ref[:, :D]
        keep_ref[start : start + count, 2 * HID_DEV :] = ref[:, D:].astype(f32)
        start += count
    pieces = jnp.concatenate([own_w_ref[D:, :], other_w_ref[D:, :]], axis=1).astype(f32)
    proj = pieces[0:1] + pieces[1:2] + pieces[2:3]
    pre = jnp.dot(x_ref[...], u_ref[...], preferred_element_type=f32)
    sig = jax.nn.sigmoid(pre)
    hidden = (pre * sig).astype(bf16)
    keep_ref[:ROWS, : 2 * HID_DEV] = pre
    keep_ref[ROWS:, : 2 * HID_DEV] = jnp.broadcast_to(proj, (8, 2 * HID_DEV))
    value = jnp.sum(hidden.astype(f32) * proj, axis=1, keepdims=True)
    lane = iota((CAP, 128), 1)
    token = iota((CAP, TOK_DEV), 1).astype(f32)
    row = iota((16, TOK_DEV), 0)
    total = jnp.where((row == zh * 4 + y) & (grp == 0), base_ref[0:1, :], 0.0)
    for at, k, d in BLOCKS:
        note = keep_ref[at : at + CAP, 2 * HID_DEV :]
        gate = jnp.sum(jnp.where((lane >= 1 + 3 * zh) & (lane < 4 + 3 * zh), note, 0.0), axis=1, keepdims=True)
        term = gate * value[at : at + CAP]
        spread = jnp.sum(jnp.where(note[:, 0:1] == token, term, 0.0), axis=0, keepdims=True)
        total = total + jnp.where(row == (zh ^ k) * 4 + (y ^ d), spread, 0.0)
    part_ref[...] = total


def backward_kernel(info_ref, table_ref, x_ref, keep_ref, own_ref, send_ref, own_head_ref):
    zh, c, y = info_ref[1], info_ref[4], info_ref[3]
    table = table_ref[...]
    note = keep_ref[:ROWS, 2 * HID_DEV :]
    token = iota((CAP, TOK_DEV), 1).astype(f32)
    lane = iota((CAP, 128), 1)
    mine, gates = [], []
    for at, k, d in BLOCKS:
        block = ((zh ^ k) * 4 + (y ^ d)) * 2 + c
        values = table_ref[pl.ds(block, 1), :]
        part = keep_ref[at : at + CAP, 2 * HID_DEV :]
        mine.append(jnp.sum(jnp.where(part[:, 0:1] == token, values, 0.0), axis=1, keepdims=True))
        gates.append(
            jnp.sum(jnp.where((lane >= 1 + 3 * zh) & (lane < 4 + 3 * zh), part, 0.0), axis=1, keepdims=True)
        )
    mine = jnp.concatenate(mine, axis=0)
    gate = jnp.concatenate(gates, axis=0)
    hot = jnp.where(iota((ROWS, 32), 1).astype(f32) == note[:, 13:14], 1.0, 0.0).astype(bf16)
    found = jnp.zeros((ROWS, TOK_DEV), f32)
    for part in thirds(table):
        found = found + jnp.dot(hot, part.astype(bf16), preferred_element_type=f32)
    places = iota((ROWS, TOK_DEV), 1).astype(f32)
    theirs = jnp.sum(jnp.where(places == note[:, 14:15], found, 0.0), axis=1, keepdims=True)
    side = note[:, 15:16]
    margin = side * (mine - theirs)
    grad = -side * (64.0 * jax.nn.sigmoid(-margin)) * gate
    pre = keep_ref[:ROWS, : 2 * HID_DEV]
    proj = keep_ref[ROWS : ROWS + 1, : 2 * HID_DEV]
    sig = jax.nn.sigmoid(pre)
    hidden = (pre * sig).astype(bf16).astype(f32)
    hid_grad = jnp.sum(grad * hidden, axis=0, keepdims=True)
    pre_grad = (grad * proj * (sig * (1.0 + pre * (1.0 - sig)))).astype(bf16)
    out = lax.dot_general(x_ref[...], pre_grad, (((0,), (0,)), ((), ())), preferred_element_type=f32)
    own_ref[...] = out[:, :HID_DEV]
    send_ref[:D, :] = out[:, HID_DEV:]
    own_head_ref[...] = jnp.broadcast_to(hid_grad[:, :HID_DEV], (8, HID_DEV))
    send_ref[D:, :] = jnp.broadcast_to(hid_grad[:, HID_DEV:], (8, HID_DEV))


def loss_kernel(table_ref, pair_ref, out_ref):
    parts = jnp.concatenate([p.astype(bf16) for p in thirds(table_ref[...])], axis=0)

    def rewards_of(index):
        high = jnp.floor(index * (1.0 / TOK_DEV))
        low = index - high * TOK_DEV
        count = index.shape[1]
        row = iota((96, count), 0) & 31
        hot = jnp.where(row.astype(f32) == high, 1.0, 0.0).astype(bf16)
        found = lax.dot_general(parts, hot, (((0,), (0,)), ((), ())), preferred_element_type=f32)
        return jnp.sum(jnp.where(iota((TOK_DEV, count), 0).astype(f32) == low, found, 0.0), axis=0, keepdims=True)

    def step(r, total):
        def line(at):
            rows = [pair_ref[pl.ds(at + i, 1), :].astype(f32) for i in range(4)]
            return jnp.concatenate(rows, axis=1)

        margin = rewards_of(line(4 * r)) - rewards_of(line(4 * r + 32))
        return total + jnp.maximum(-margin, 0.0) + jnp.log1p(jnp.exp(-jnp.abs(margin)))

    total = lax.fori_loop(0, 8, step, jnp.zeros((1, 512), f32))
    out_ref[...] = jnp.broadcast_to(jnp.sum(total, axis=1, keepdims=True) * (1.0 / PAIRS), (1, 128))


def final_kernel(
    take_ref, up_ref, up_got_ref, down_ref, down_got_ref, own_ref, recv_ref, own_head_ref, head_ref, new_up_ref, new_down_ref
):
    step = own_ref[...] + recv_ref[:D, :]
    grad = own_head_ref[0:1] + recv_ref[D : D + 1, :]
    square = (HID_DEV, HID_DEV)
    column = jnp.sum(jnp.where(iota(square, 0) == iota(square, 1), grad, 0.0), axis=1, keepdims=True)
    head = head_ref[...].astype(f32)
    for wanted, ref in ((1, up_got_ref), (0, up_ref)):

        @pl.when(take_ref[0] == wanted)
        def _(ref=ref):
            new_up_ref[...] = (ref[...].astype(f32) + step).astype(bf16)

    for wanted, ref in ((1, down_got_ref), (0, down_ref)):

        @pl.when(take_ref[1] == wanted)
        def _(ref=ref):
            for j in range(D // HID_DEV):
                at = j * HID_DEV
                old = ref[at : at + HID_DEV, :].astype(f32)
                new_down_ref[:, at : at + HID_DEV] = (old + column * head[j : j + 1]).astype(bf16)


def pick_kernel(count, take_ref, *refs):
    got_refs, own_refs, out_refs = refs[:count], refs[count : 2 * count], refs[-count:]
    for i in range(count):

        @pl.when(take_ref[i] == 1)
        def _(i=i):
            out_refs[i][...] = got_refs[i][...]

        @pl.when(take_ref[i] == 0)
        def _(i=i):
            out_refs[i][...] = own_refs[i][...]


def split_kernel(take_ref, got_ref, own_ref, earlier_ref, up_ref, down_ref):
    for wanted, ref in ((1, got_ref), (0, own_ref)):

        @pl.when(take_ref[0] == wanted)
        def _(ref=ref):
            up_ref[...] = ref[:D, :]
            down_ref[...] = ref[D:, :]


def others_kernel(info_ref, rows_ref, *refs):
    zh = info_ref[1]
    for k in range(1, EXP_GRP):
        block = rows_ref[pl.ds(pl.multiple_of((zh ^ k) * CAP, CAP), CAP), :]
        refs[-1][CAP * (k - 1) : CAP * k, :] = block


def swap(block, axis, mask):
    count = lax.axis_size(axis)
    return lax.ppermute(block, axis, [(i, i ^ mask) for i in range(count)])


def picks(stages, got, own, *earlier):
    count = len(stages)
    return pl.pallas_call(
        functools.partial(pick_kernel, count),
        out_shape=[shape(o.shape, o.dtype) for o in own],
        in_specs=[SMEM] + [VMEM] * (2 * count) + [ANY] * len(earlier),
        out_specs=[VMEM] * count,
        compiler_params=PARAMS,
        cost_estimate=LIGHT,
        name="pick",
    )(jnp.concatenate([s[2] for s in stages]), *got, *own, *earlier)


def pick(stage, got, own, *earlier):
    return picks([stage], [got], [own], *earlier)[0]


def others(info, rows, *earlier):
    return pl.pallas_call(
        others_kernel,
        out_shape=shape((3 * CAP, WIDE), bf16),
        in_specs=[SMEM, VMEM] + [ANY] * len(earlier),
        out_specs=VMEM,
        compiler_params=PARAMS,
        cost_estimate=SPACED,
        name="others",
    )(info, rows, *earlier)


def body(tokens, routes, gate_values, old_group, move_mask, pair_index, reward_head, w_up, w_down, acc_up, acc_down):
    x, zl, zh, y, c = (lax.axis_index(a) for a in ("x", "zl", "zh", "y", "c"))
    info = jnp.stack([x * 4 + zl, zh, zh * 8 + y * 2 + c, y, c]).astype(jnp.int32)
    head = reward_head.reshape(D // 128, 128)
    pairs = pair_index.reshape(64, 128)
    mask = jnp.sum(jnp.where(jnp.arange(EXP_GRP) == zh, move_mask, 0))
    bit = [jnp.bitwise_and(jnp.right_shift(mask, i), 1) for i in range(4)]
    x1 = ("x", 1, jnp.bitwise_xor(bit[2], bit[3]).reshape(1))
    x3 = ("x", 3, bit[3].reshape(1))
    z1 = ("zl", 1, bit[0].reshape(1))
    z2 = ("zl", 2, bit[1].reshape(1))

    sent, own_rows, base, weights, accums = pl.pallas_call(
        dispatch_kernel,
        out_shape=[
            shape((EXP_GRP * CAP, WIDE), bf16),
            shape((CAP, WIDE), bf16),
            shape((8, TOK_DEV), f32),
            shape((D + 16, HID_DEV), bf16),
            shape((2 * D, HID_DEV), bf16),
        ],
        in_specs=[SMEM] * 3 + [VMEM] * 9,
        out_specs=[VMEM] * 5,
        compiler_params=pltpu.CompilerParams(vmem_limit_bytes=63 * 1024 * 1024),
        name="dispatch",
    )(
        old_group,
        move_mask,
        info,
        tokens,
        routes.T,
        gate_values.T,
        pairs,
        head,
        w_up[0],
        w_down[0],
        acc_up[0],
        acc_down[0],
    )
    arrived = lax.all_to_all(sent, "zh", 0, 0, tiled=True)
    got = swap(weights, *x1[:2])
    weights = pick(x1, got, weights)
    weights, own_rows, accums = lax.optimization_barrier((weights, own_rows, accums))
    got = swap(weights, *x3[:2])
    held = [own_rows] + [swap(own_rows, "y", d) for d in (1, 2, 3)]
    acc_got = swap(accums, *x1[:2])
    weights = pick(x3, got, weights)
    got = swap(weights, *z1[:2])
    accums = pick(x1, acc_got, accums, weights)
    acc_got = swap(accums, *x3[:2])
    weights = pick(z1, got, weights, accums, *held[1:])
    got = swap(weights, *z2[:2])
    rows = others(info, arrived, weights)
    held += [rows] + [swap(rows, "y", d) for d in (1, 2, 3)]
    weights = pick(z2, got, weights, rows)
    other_weights = swap(weights, "c", 1)
    up, down = pl.pallas_call(
        split_kernel,
        out_shape=[shape((D, HID_DEV), bf16)] * 2,
        in_specs=[SMEM, VMEM, VMEM, ANY],
        out_specs=[VMEM] * 2,
        compiler_params=PARAMS,
        cost_estimate=SPACED,
        name="pick_split",
    )(x3[2], acc_got, accums, weights)
    up_got = swap(up, *z1[:2])
    down_got = swap(down, *z2[:2])

    xs, keep, part = pl.pallas_call(
        forward_kernel,
        out_shape=[
            shape((ROWS, D), bf16),
            shape((ROWS + 8, 2 * HID_DEV + 128), f32),
            shape((16, TOK_DEV), f32),
        ],
        in_specs=[SMEM] + [VMEM] * 11,
        out_specs=[VMEM] * 3,
        scratch_shapes=[pltpu.VMEM((D, 2 * HID_DEV), bf16)],
        compiler_params=PARAMS,
        name="forward",
    )(info, base, weights, other_weights, *held)

    mine = lax.all_to_all(part, ("x", "y"), 0, 0, tiled=True)
    mine = jnp.broadcast_to(jnp.sum(mine, axis=0, keepdims=True), (16, TOK_DEV))
    mine = lax.all_to_all(mine, ("zl", "zh"), 0, 0, tiled=True)
    mine = jnp.broadcast_to(jnp.sum(mine, axis=0, keepdims=True), (32, TOK_DEV))
    up, down = picks([z1, z2], [up_got, down_got], [up, down], mine)
    mine, up, down = lax.optimization_barrier((mine, up, down))
    up_got = swap(up, *z2[:2])
    down_got = swap(down, *z1[:2])
    table = lax.all_to_all(mine, ("x", "y", "c"), 0, 0, tiled=True)

    own, send, own_head = pl.pallas_call(
        backward_kernel,
        out_shape=[shape((D, HID_DEV), f32), shape((D + 8, HID_DEV), f32), shape((8, HID_DEV), f32)],
        in_specs=[SMEM] + [VMEM] * 3,
        out_specs=[VMEM] * 3,
        compiler_params=PARAMS,
        cost_estimate=SPACED,
        name="backward",
    )(info, table, xs, keep)
    recv = swap(send, "c", 1)
    loss = pl.pallas_call(
        loss_kernel,
        out_shape=shape((1, 128), f32),
        in_specs=[VMEM] * 2,
        out_specs=VMEM,
        compiler_params=PARAMS,
        cost_estimate=SPACED,
        name="loss",
    )(table, pairs)
    new_up, new_down = pl.pallas_call(
        final_kernel,
        out_shape=[shape((D, HID_DEV), bf16), shape((HID_DEV, D), bf16)],
        in_specs=[SMEM] + [VMEM] * 8,
        out_specs=[VMEM] * 2,
        compiler_params=PARAMS,
        name="final",
    )(jnp.concatenate([z2[2], z1[2]]), up, up_got, down, down_got, own, recv, own_head, head)
    return new_up[None], new_down[None], loss[0, 0]


def solution(mesh):
    fine = Mesh(mesh.devices.reshape(4, 4, 4, 4, 2), ("x", "zl", "zh", "y", "c"))
    grp, ep = ("x", "zl"), ("zh", "y", "c")
    return jax.shard_map(
        body,
        mesh=fine,
        in_specs=(P(ep, None), P(ep, None), P(ep, None), P(), P(), P(), P())
        + (P(grp, None, ep), P(grp, ep, None)) * 2,
        out_specs=(P(grp, None, ep), P(grp, ep, None), P()),
        check_vma=False,
    )
```

```python
import functools

import jax
import jax.numpy as jnp
from jax import lax
from jax.experimental import pallas as pl
from jax.experimental.pallas import tpu as pltpu
from jax.sharding import Mesh
from jax.sharding import PartitionSpec as P

D = 2048
HID_DEV = 128
EXP_GRP = 4
TOK_DEV = 256
CAP = 48
WIDE = D + 128
ROWS = 16 * CAP
PAIRS = 4096

f32 = jnp.float32
bf16 = jnp.bfloat16
VMEM = pl.BlockSpec(memory_space=pltpu.VMEM)
SMEM = pl.BlockSpec(memory_space=pltpu.SMEM)
PARAMS = pltpu.CompilerParams(vmem_limit_bytes=24 * 1024 * 1024)
NT = (((1,), (1,)), ((), ()))

BLOCKS = [(CAP * d, 0, d) for d in range(4)] + [
    (4 * CAP + 3 * CAP * d + CAP * (k - 1), k, d) for d in range(4) for k in range(1, EXP_GRP)
]
LIGHT = pl.CostEstimate(flops=0, bytes_accessed=0, transcendentals=0)
SPACED = pl.CostEstimate(flops=10**11, bytes_accessed=0, transcendentals=0)
ANY = pl.BlockSpec(memory_space=pl.ANY)


def shape(dims, kind):
    return jax.ShapeDtypeStruct(dims, kind)


def iota(dims, axis):
    return lax.broadcasted_iota(jnp.int32, dims, axis)


def thirds(value):
    first = value.astype(bf16).astype(f32)
    second = (value - first).astype(bf16).astype(f32)
    third = (value - first - second).astype(bf16).astype(f32)
    return first, second, third


def dispatch_kernel(
    group_ref,
    mask_ref,
    info_ref,
    tok_ref,
    routes_ref,
    gates_ref,
    pair_ref,
    head_ref,
    up_ref,
    down_ref,
    acc_up_ref,
    acc_down_ref,
    *outs,
):
    out_ref, own_ref, base_ref, weights_ref, acc_ref = outs
    acc_ref[:D, :] = acc_up_ref[...]
    for j in range(D // HID_DEV):
        at = j * HID_DEV
        acc_ref[D + at : D + at + HID_DEV, :] = acc_down_ref[:, at : at + HID_DEV]
    weights_ref[:D, :] = up_ref[...]
    head = head_ref[...].astype(f32)
    head = jnp.concatenate([head[j : j + 1] for j in range(D // 128)], axis=1)
    head = jnp.broadcast_to(head, (16, D)).astype(bf16)
    proj = lax.dot_general(head, down_ref[...], NT, preferred_element_type=f32)
    first, second, third = thirds(proj)
    row = iota((16, HID_DEV), 0)
    packed = jnp.where(row == 0, first, jnp.where(row == 1, second, jnp.where(row == 2, third, 0.0)))
    weights_ref[D:, :] = packed.astype(bf16)
    grp, zh, member = info_ref[0], info_ref[1], info_ref[2]
    routes = routes_ref[...]
    gates = gates_ref[...]
    sel, gate = [], []
    for k in range(EXP_GRP):
        slot = k
        mask = mask_ref[slot]
        expert = jnp.int32(0)
        for j in range(16):
            found = (group_ref[4 * j + slot] ^ mask) == grp
            expert = jnp.where(found, 4 * j + slot, expert)
        hit = routes == expert
        sel.append(jnp.sum(jnp.where(hit, 1.0, 0.0), axis=0, keepdims=True))
        gate.append(jnp.sum(jnp.where(hit, gates, 0.0), axis=0, keepdims=True))
    row8 = iota((8, TOK_DEV), 0)
    chosen = jnp.zeros((8, TOK_DEV), f32)
    for k in range(EXP_GRP):
        chosen = jnp.where(row8 == k, sel[k], chosen)
    tri = jnp.where(iota((TOK_DEV, TOK_DEV), 0) <= iota((TOK_DEV, TOK_DEV), 1), 1.0, 0.0).astype(bf16)
    place = jnp.dot(chosen.astype(bf16), tri, preferred_element_type=f32) - 1.0
    own = (iota((TOK_DEV, 1), 0) + member * TOK_DEV).astype(f32)

    def look(r, code):
        first = pair_ref[pl.ds(r, 1), :].astype(f32)
        second = pair_ref[pl.ds(r + 32, 1), :].astype(f32)
        return jnp.where(first == own, second + 1.0, jnp.where(second == own, -1.0 - first, code))

    code = lax.fori_loop(0, 32, look, jnp.zeros((TOK_DEV, 128), f32), unroll=4)
    code = jnp.sum(code, axis=1, keepdims=True)
    partner = jnp.abs(code) - 1.0
    high = jnp.floor(partner * (1.0 / TOK_DEV))
    low = partner - high * TOK_DEV
    lane = iota((TOK_DEV, 128), 1)
    by_token = jnp.where(lane == 13, high, jnp.where(lane == 14, low, jnp.where(lane == 15, jnp.where(code > 0, 1.0, -1.0), 0.0)))
    by_token = jnp.where(lane == 0, iota((TOK_DEV, 128), 0).astype(f32), by_token).astype(bf16)
    rows = iota((128, TOK_DEV), 0)
    by_slot = jnp.zeros((128, TOK_DEV), f32)
    for k in range(EXP_GRP):
        for j, part in enumerate(thirds(gate[k])):
            by_slot = jnp.where(rows == 1 + 3 * k + j, part, by_slot)
    by_slot = by_slot.astype(bf16)
    base_ref[...] = lax.dot_general(head, tok_ref[...], NT, preferred_element_type=f32)[:8]
    height = iota((CAP, TOK_DEV), 0).astype(f32)
    picks = [
        jnp.where((place[k : k + 1] == height) & (sel[k] > 0.5), 1.0, 0.0).astype(bf16) for k in range(EXP_GRP)
    ]
    pick = jnp.concatenate(picks, axis=0)
    notes = jnp.dot(pick, by_token, preferred_element_type=f32) + lax.dot_general(
        pick, by_slot, NT, preferred_element_type=f32
    )
    wide = jnp.dot(pick, tok_ref[...], preferred_element_type=f32)
    out_ref[:, :D] = wide.astype(bf16)
    out_ref[:, D:] = notes.astype(bf16)
    own_ref[...] = out_ref[pl.ds(pl.multiple_of(zh * CAP, CAP), CAP), :]


def forward_kernel(info_ref, base_ref, own_w_ref, other_w_ref, *refs):
    groups, (x_ref, keep_ref, part_ref, u_ref) = refs[:8], refs[8:]
    grp, zh, y = info_ref[0], info_ref[1], info_ref[3]
    u_ref[:, :HID_DEV] = own_w_ref[:D, :]
    u_ref[:, HID_DEV:] = other_w_ref[:D, :]
    start = 0
    for ref in groups:
        count = ref.shape[0]
        x_ref[start : start + count, :] = ref[:, :D]
        keep_ref[start : start + count, 2 * HID_DEV :] = ref[:, D:].astype(f32)
        start += count
    pieces = jnp.concatenate([own_w_ref[D:, :], other_w_ref[D:, :]], axis=1).astype(f32)
    proj = pieces[0:1] + pieces[1:2] + pieces[2:3]
    pre = jnp.dot(x_ref[...], u_ref[...], preferred_element_type=f32)
    sig = jax.nn.sigmoid(pre)
    hidden = (pre * sig).astype(bf16)
    keep_ref[:ROWS, : 2 * HID_DEV] = pre
    keep_ref[ROWS:, : 2 * HID_DEV] = jnp.broadcast_to(proj, (8, 2 * HID_DEV))
    value = jnp.sum(hidden.astype(f32) * proj, axis=1, keepdims=True)
    lane = iota((CAP, 128), 1)
    token = iota((CAP, TOK_DEV), 1).astype(f32)
    row = iota((16, TOK_DEV), 0)
    total = jnp.where((row == zh * 4 + y) & (grp == 0), base_ref[0:1, :], 0.0)
    for at, k, d in BLOCKS:
        note = keep_ref[at : at + CAP, 2 * HID_DEV :]
        gate = jnp.sum(jnp.where((lane >= 1 + 3 * zh) & (lane < 4 + 3 * zh), note, 0.0), axis=1, keepdims=True)
        term = gate * value[at : at + CAP]
        spread = jnp.sum(jnp.where(note[:, 0:1] == token, term, 0.0), axis=0, keepdims=True)
        total = total + jnp.where(row == (zh ^ k) * 4 + (y ^ d), spread, 0.0)
    part_ref[...] = total


def backward_kernel(info_ref, table_ref, x_ref, keep_ref, own_ref, send_ref, own_head_ref):
    zh, c, y = info_ref[1], info_ref[4], info_ref[3]
    table = table_ref[...]
    note = keep_ref[:ROWS, 2 * HID_DEV :]
    token = iota((CAP, TOK_DEV), 1).astype(f32)
    lane = iota((CAP, 128), 1)
    mine, gates = [], []
    for at, k, d in BLOCKS:
        block = ((zh ^ k) * 4 + (y ^ d)) * 2 + c
        values = table_ref[pl.ds(block, 1), :]
        part = keep_ref[at : at + CAP, 2 * HID_DEV :]
        mine.append(jnp.sum(jnp.where(part[:, 0:1] == token, values, 0.0), axis=1, keepdims=True))
        gates.append(
            jnp.sum(jnp.where((lane >= 1 + 3 * zh) & (lane < 4 + 3 * zh), part, 0.0), axis=1, keepdims=True)
        )
    mine = jnp.concatenate(mine, axis=0)
    gate = jnp.concatenate(gates, axis=0)
    hot = jnp.where(iota((ROWS, 32), 1).astype(f32) == note[:, 13:14], 1.0, 0.0).astype(bf16)
    found = jnp.zeros((ROWS, TOK_DEV), f32)
    for part in thirds(table):
        found = found + jnp.dot(hot, part.astype(bf16), preferred_element_type=f32)
    places = iota((ROWS, TOK_DEV), 1).astype(f32)
    theirs = jnp.sum(jnp.where(places == note[:, 14:15], found, 0.0), axis=1, keepdims=True)
    side = note[:, 15:16]
    margin = side * (mine - theirs)
    grad = -side * (64.0 * jax.nn.sigmoid(-margin)) * gate
    pre = keep_ref[:ROWS, : 2 * HID_DEV]
    proj = keep_ref[ROWS : ROWS + 1, : 2 * HID_DEV]
    sig = jax.nn.sigmoid(pre)
    hidden = (pre * sig).astype(bf16).astype(f32)
    hid_grad = jnp.sum(grad * hidden, axis=0, keepdims=True)
    pre_grad = (grad * proj * (sig * (1.0 + pre * (1.0 - sig)))).astype(bf16)
    out = lax.dot_general(x_ref[...], pre_grad, (((0,), (0,)), ((), ())), preferred_element_type=f32)
    own_ref[...] = out[:, :HID_DEV]
    send_ref[:D, :] = out[:, HID_DEV:]
    own_head_ref[...] = jnp.broadcast_to(hid_grad[:, :HID_DEV], (8, HID_DEV))
    send_ref[D:, :] = jnp.broadcast_to(hid_grad[:, HID_DEV:], (8, HID_DEV))


def loss_kernel(table_ref, pair_ref, out_ref):
    parts = jnp.concatenate([p.astype(bf16) for p in thirds(table_ref[...])], axis=0)

    def rewards_of(index):
        high = jnp.floor(index * (1.0 / TOK_DEV))
        low = index - high * TOK_DEV
        count = index.shape[1]
        row = iota((96, count), 0) & 31
        hot = jnp.where(row.astype(f32) == high, 1.0, 0.0).astype(bf16)
        found = lax.dot_general(parts, hot, (((0,), (0,)), ((), ())), preferred_element_type=f32)
        return jnp.sum(jnp.where(iota((TOK_DEV, count), 0).astype(f32) == low, found, 0.0), axis=0, keepdims=True)

    def step(r, total):
        def line(at):
            rows = [pair_ref[pl.ds(at + i, 1), :].astype(f32) for i in range(4)]
            return jnp.concatenate(rows, axis=1)

        margin = rewards_of(line(4 * r)) - rewards_of(line(4 * r + 32))
        return total + jnp.maximum(-margin, 0.0) + jnp.log1p(jnp.exp(-jnp.abs(margin)))

    total = lax.fori_loop(0, 8, step, jnp.zeros((1, 512), f32))
    out_ref[...] = jnp.broadcast_to(jnp.sum(total, axis=1, keepdims=True) * (1.0 / PAIRS), (1, 128))


def final_kernel(
    take_ref, up_ref, up_got_ref, down_ref, down_got_ref, own_ref, recv_ref, own_head_ref, head_ref, new_up_ref, new_down_ref
):
    step = own_ref[...] + recv_ref[:D, :]
    grad = own_head_ref[0:1] + recv_ref[D : D + 1, :]
    square = (HID_DEV, HID_DEV)
    column = jnp.sum(jnp.where(iota(square, 0) == iota(square, 1), grad, 0.0), axis=1, keepdims=True)
    head = head_ref[...].astype(f32)
    for wanted, ref in ((1, up_got_ref), (0, up_ref)):

        @pl.when(take_ref[0] == wanted)
        def _(ref=ref):
            new_up_ref[...] = (ref[...].astype(f32) + step).astype(bf16)

    for wanted, ref in ((1, down_got_ref), (0, down_ref)):

        @pl.when(take_ref[1] == wanted)
        def _(ref=ref):
            for j in range(D // HID_DEV):
                at = j * HID_DEV
                old = ref[at : at + HID_DEV, :].astype(f32)
                new_down_ref[:, at : at + HID_DEV] = (old + column * head[j : j + 1]).astype(bf16)


def pick_kernel(count, take_ref, *refs):
    got_refs, own_refs, out_refs = refs[:count], refs[count : 2 * count], refs[-count:]
    for i in range(count):

        @pl.when(take_ref[i] == 1)
        def _(i=i):
            out_refs[i][...] = got_refs[i][...]

        @pl.when(take_ref[i] == 0)
        def _(i=i):
            out_refs[i][...] = own_refs[i][...]


def split_kernel(take_ref, got_ref, own_ref, earlier_ref, up_ref, down_ref):
    for wanted, ref in ((1, got_ref), (0, own_ref)):

        @pl.when(take_ref[0] == wanted)
        def _(ref=ref):
            up_ref[...] = ref[:D, :]
            down_ref[...] = ref[D:, :]


def others_kernel(info_ref, rows_ref, *refs):
    zh = info_ref[1]
    for k in range(1, EXP_GRP):
        block = rows_ref[pl.ds(pl.multiple_of((zh ^ k) * CAP, CAP), CAP), :]
        refs[-1][CAP * (k - 1) : CAP * k, :] = block


def swap(block, axis, mask):
    count = lax.axis_size(axis)
    return lax.ppermute(block, axis, [(i, i ^ mask) for i in range(count)])


def picks(stages, got, own, *earlier, cost=LIGHT):
    count = len(stages)
    return pl.pallas_call(
        functools.partial(pick_kernel, count),
        out_shape=[shape(o.shape, o.dtype) for o in own],
        in_specs=[SMEM] + [VMEM] * (2 * count) + [ANY] * len(earlier),
        out_specs=[VMEM] * count,
        compiler_params=PARAMS,
        cost_estimate=cost,
        name="pick",
    )(jnp.concatenate([s[2] for s in stages]), *got, *own, *earlier)


def pick(stage, got, own, *earlier, cost=LIGHT):
    return picks([stage], [got], [own], *earlier, cost=cost)[0]


def others(info, rows, *earlier):
    return pl.pallas_call(
        others_kernel,
        out_shape=shape((3 * CAP, WIDE), bf16),
        in_specs=[SMEM, VMEM] + [ANY] * len(earlier),
        out_specs=VMEM,
        compiler_params=PARAMS,
        cost_estimate=SPACED,
        name="others",
    )(info, rows, *earlier)


def body(tokens, routes, gate_values, old_group, move_mask, pair_index, reward_head, w_up, w_down, acc_up, acc_down):
    x, zl, zh, y, c = (lax.axis_index(a) for a in ("x", "zl", "zh", "y", "c"))
    info = jnp.stack([x * 4 + zl, zh, zh * 8 + y * 2 + c, y, c]).astype(jnp.int32)
    head = reward_head.reshape(D // 128, 128)
    pairs = pair_index.reshape(64, 128)
    mask = jnp.sum(jnp.where(jnp.arange(EXP_GRP) == zh, move_mask, 0))
    bit = [jnp.bitwise_and(jnp.right_shift(mask, i), 1) for i in range(4)]
    x1 = ("x", 1, jnp.bitwise_xor(bit[2], bit[3]).reshape(1))
    x3 = ("x", 3, bit[3].reshape(1))
    z1 = ("zl", 1, bit[0].reshape(1))
    z2 = ("zl", 2, bit[1].reshape(1))

    sent, own_rows, base, weights, accums = pl.pallas_call(
        dispatch_kernel,
        out_shape=[
            shape((EXP_GRP * CAP, WIDE), bf16),
            shape((CAP, WIDE), bf16),
            shape((8, TOK_DEV), f32),
            shape((D + 16, HID_DEV), bf16),
            shape((2 * D, HID_DEV), bf16),
        ],
        in_specs=[SMEM] * 3 + [VMEM] * 9,
        out_specs=[VMEM] * 5,
        compiler_params=pltpu.CompilerParams(vmem_limit_bytes=63 * 1024 * 1024),
        name="dispatch",
    )(
        old_group,
        move_mask,
        info,
        tokens,
        routes.T,
        gate_values.T,
        pairs,
        head,
        w_up[0],
        w_down[0],
        acc_up[0],
        acc_down[0],
    )
    arrived = lax.all_to_all(sent, "zh", 0, 0, tiled=True)
    got = swap(weights, *x1[:2])
    weights = pick(x1, got, weights)
    weights, own_rows, accums = lax.optimization_barrier((weights, own_rows, accums))
    got = swap(weights, *x3[:2])
    held = [own_rows] + [swap(own_rows, "y", d) for d in (1, 2, 3)]
    acc_got = swap(accums, *x1[:2])
    weights = pick(x3, got, weights, *held[1:])
    got = swap(weights, *z1[:2])
    accums = pick(x1, acc_got, accums, weights)
    acc_got = swap(accums, *x3[:2])
    rows = others(info, arrived, weights, accums)
    held += [rows] + [swap(rows, "y", d) for d in (1, 2, 3)]
    weights = pick(z1, got, weights, rows, cost=SPACED)
    got = swap(weights, *z2[:2])
    weights = pick(z2, got, weights)
    other_weights = swap(weights, "c", 1)
    up, down = pl.pallas_call(
        split_kernel,
        out_shape=[shape((D, HID_DEV), bf16)] * 2,
        in_specs=[SMEM, VMEM, VMEM, ANY],
        out_specs=[VMEM] * 2,
        compiler_params=PARAMS,
        cost_estimate=SPACED,
        name="pick_split",
    )(x3[2], acc_got, accums, weights)
    up_got = swap(up, *z1[:2])
    down_got = swap(down, *z2[:2])

    xs, keep, part = pl.pallas_call(
        forward_kernel,
        out_shape=[
            shape((ROWS, D), bf16),
            shape((ROWS + 8, 2 * HID_DEV + 128), f32),
            shape((16, TOK_DEV), f32),
        ],
        in_specs=[SMEM] + [VMEM] * 11,
        out_specs=[VMEM] * 3,
        scratch_shapes=[pltpu.VMEM((D, 2 * HID_DEV), bf16)],
        compiler_params=PARAMS,
        name="forward",
    )(info, base, weights, other_weights, *held)

    mine = lax.all_to_all(part, ("x", "y"), 0, 0, tiled=True)
    up, down = picks([z1, z2], [up_got, down_got], [up, down], mine)
    mine, up, down = lax.optimization_barrier((mine, up, down))
    up_got = swap(up, *z2[:2])
    down_got = swap(down, *z1[:2])
    mine = jnp.broadcast_to(jnp.sum(mine, axis=0, keepdims=True), (16, TOK_DEV))
    mine = lax.all_to_all(mine, ("zl", "zh"), 0, 0, tiled=True)
    mine = jnp.broadcast_to(jnp.sum(mine, axis=0, keepdims=True), (32, TOK_DEV))
    table = lax.all_to_all(mine, ("x", "y", "c"), 0, 0, tiled=True)

    table, up_got, down_got = lax.optimization_barrier((table, up_got, down_got))
    own, send, own_head = pl.pallas_call(
        backward_kernel,
        out_shape=[shape((D, HID_DEV), f32), shape((D + 8, HID_DEV), f32), shape((8, HID_DEV), f32)],
        in_specs=[SMEM] + [VMEM] * 3,
        out_specs=[VMEM] * 3,
        compiler_params=PARAMS,
        cost_estimate=SPACED,
        name="backward",
    )(info, table, xs, keep)
    recv = swap(send, "c", 1)
    loss = pl.pallas_call(
        loss_kernel,
        out_shape=shape((1, 128), f32),
        in_specs=[VMEM] * 2,
        out_specs=VMEM,
        compiler_params=PARAMS,
        cost_estimate=SPACED,
        name="loss",
    )(table, pairs)
    new_up, new_down = pl.pallas_call(
        final_kernel,
        out_shape=[shape((D, HID_DEV), bf16), shape((HID_DEV, D), bf16)],
        in_specs=[SMEM] + [VMEM] * 8,
        out_specs=[VMEM] * 2,
        compiler_params=PARAMS,
        name="final",
    )(jnp.concatenate([z2[2], z1[2]]), up, up_got, down, down_got, own, recv, own_head, head)
    return new_up[None], new_down[None], loss[0, 0]


def solution(mesh):
    fine = Mesh(mesh.devices.reshape(4, 4, 4, 4, 2), ("x", "zl", "zh", "y", "c"))
    grp, ep = ("x", "zl"), ("zh", "y", "c")
    return jax.shard_map(
        body,
        mesh=fine,
        in_specs=(P(ep, None), P(ep, None), P(ep, None), P(), P(), P(), P())
        + (P(grp, None, ep), P(grp, ep, None)) * 2,
        out_specs=(P(grp, None, ep), P(grp, ep, None), P()),
        check_vma=False,
    )
```

```python
import functools

import jax
import jax.numpy as jnp
from jax import lax
from jax.experimental import pallas as pl
from jax.experimental.pallas import tpu as pltpu
from jax.sharding import Mesh
from jax.sharding import PartitionSpec as P

D = 2048
HID_DEV = 128
EXP_GRP = 4
TOK_DEV = 256
CAP = 48
WIDE = D + 128
ROWS = 16 * CAP
PAIRS = 4096

f32 = jnp.float32
bf16 = jnp.bfloat16
VMEM = pl.BlockSpec(memory_space=pltpu.VMEM)
SMEM = pl.BlockSpec(memory_space=pltpu.SMEM)
WHOLE = pltpu.CompilerParams(vmem_limit_bytes=62 * 1024 * 1024)
PARAMS = pltpu.CompilerParams(vmem_limit_bytes=24 * 1024 * 1024)
NT = (((1,), (1,)), ((), ()))

BLOCKS = [(CAP * d, 0, d) for d in range(4)] + [
    (4 * CAP + 3 * CAP * d + CAP * (k - 1), k, d) for d in range(4) for k in range(1, EXP_GRP)
]
LIGHT = pl.CostEstimate(flops=0, bytes_accessed=0, transcendentals=0)
SPACED = pl.CostEstimate(flops=10**11, bytes_accessed=0, transcendentals=0)
ANY = pl.BlockSpec(memory_space=pl.ANY)


def shape(dims, kind):
    return jax.ShapeDtypeStruct(dims, kind)


def iota(dims, axis):
    return lax.broadcasted_iota(jnp.int32, dims, axis)


def thirds(value):
    first = value.astype(bf16).astype(f32)
    second = (value - first).astype(bf16).astype(f32)
    third = (value - first - second).astype(bf16).astype(f32)
    return first, second, third


def dispatch_kernel(
    group_ref,
    mask_ref,
    info_ref,
    tok_ref,
    routes_ref,
    gates_ref,
    pair_ref,
    head_ref,
    up_ref,
    down_ref,
    acc_up_ref,
    acc_down_ref,
    *outs,
):
    out_ref, own_ref, base_ref, weights_ref, acc_ref = outs
    acc_ref[:D, :] = acc_up_ref[...]
    for j in range(D // HID_DEV):
        at = j * HID_DEV
        acc_ref[D + at : D + at + HID_DEV, :] = acc_down_ref[:, at : at + HID_DEV]
    weights_ref[:D, :] = up_ref[...]
    head = head_ref[...].astype(f32)
    head = jnp.concatenate([head[j : j + 1] for j in range(D // 128)], axis=1)
    head = jnp.broadcast_to(head, (16, D)).astype(bf16)
    proj = lax.dot_general(head, down_ref[...], NT, preferred_element_type=f32)
    first, second, third = thirds(proj)
    row = iota((16, HID_DEV), 0)
    packed = jnp.where(row == 0, first, jnp.where(row == 1, second, jnp.where(row == 2, third, 0.0)))
    weights_ref[D:, :] = packed.astype(bf16)
    grp, zh, member = info_ref[0], info_ref[1], info_ref[2]
    routes = routes_ref[...]
    gates = gates_ref[...]
    sel, gate = [], []
    for k in range(EXP_GRP):
        slot = k
        mask = mask_ref[slot]
        expert = jnp.int32(0)
        for j in range(16):
            found = (group_ref[4 * j + slot] ^ mask) == grp
            expert = jnp.where(found, 4 * j + slot, expert)
        hit = routes == expert
        sel.append(jnp.sum(jnp.where(hit, 1.0, 0.0), axis=0, keepdims=True))
        gate.append(jnp.sum(jnp.where(hit, gates, 0.0), axis=0, keepdims=True))
    row8 = iota((8, TOK_DEV), 0)
    chosen = jnp.zeros((8, TOK_DEV), f32)
    for k in range(EXP_GRP):
        chosen = jnp.where(row8 == k, sel[k], chosen)
    tri = jnp.where(iota((TOK_DEV, TOK_DEV), 0) <= iota((TOK_DEV, TOK_DEV), 1), 1.0, 0.0).astype(bf16)
    place = jnp.dot(chosen.astype(bf16), tri, preferred_element_type=f32) - 1.0
    own = (iota((TOK_DEV, 1), 0) + member * TOK_DEV).astype(f32)

    def look(r, code):
        first = pair_ref[pl.ds(r, 1), :].astype(f32)
        second = pair_ref[pl.ds(r + 32, 1), :].astype(f32)
        return jnp.where(first == own, second + 1.0, jnp.where(second == own, -1.0 - first, code))

    code = lax.fori_loop(0, 32, look, jnp.zeros((TOK_DEV, 128), f32), unroll=4)
    code = jnp.sum(code, axis=1, keepdims=True)
    partner = jnp.abs(code) - 1.0
    high = jnp.floor(partner * (1.0 / TOK_DEV))
    low = partner - high * TOK_DEV
    lane = iota((TOK_DEV, 128), 1)
    by_token = jnp.where(lane == 13, high, jnp.where(lane == 14, low, jnp.where(lane == 15, jnp.where(code > 0, 1.0, -1.0), 0.0)))
    by_token = jnp.where(lane == 0, iota((TOK_DEV, 128), 0).astype(f32), by_token).astype(bf16)
    rows = iota((128, TOK_DEV), 0)
    by_slot = jnp.zeros((128, TOK_DEV), f32)
    for k in range(EXP_GRP):
        for j, part in enumerate(thirds(gate[k])):
            by_slot = jnp.where(rows == 1 + 3 * k + j, part, by_slot)
    by_slot = by_slot.astype(bf16)
    base_ref[...] = lax.dot_general(head, tok_ref[...], NT, preferred_element_type=f32)[:8]
    height = iota((CAP, TOK_DEV), 0).astype(f32)
    picks = [
        jnp.where((place[k : k + 1] == height) & (sel[k] > 0.5), 1.0, 0.0).astype(bf16) for k in range(EXP_GRP)
    ]
    pick = jnp.concatenate(picks, axis=0)
    notes = jnp.dot(pick, by_token, preferred_element_type=f32) + lax.dot_general(
        pick, by_slot, NT, preferred_element_type=f32
    )
    wide = jnp.dot(pick, tok_ref[...], preferred_element_type=f32)
    out_ref[:, :D] = wide.astype(bf16)
    out_ref[:, D:] = notes.astype(bf16)
    own_ref[...] = out_ref[pl.ds(pl.multiple_of(zh * CAP, CAP), CAP), :]


def forward_kernel(info_ref, base_ref, own_w_ref, other_w_ref, *refs):
    groups, (x_ref, keep_ref, part_ref, u_ref) = refs[:8], refs[8:]
    grp, zh, y = info_ref[0], info_ref[1], info_ref[3]
    u_ref[:, :HID_DEV] = own_w_ref[:D, :]
    u_ref[:, HID_DEV:] = other_w_ref[:D, :]
    start = 0
    for ref in groups:
        count = ref.shape[0]
        x_ref[start : start + count, :] = ref[:, :D]
        keep_ref[start : start + count, 2 * HID_DEV :] = ref[:, D:].astype(f32)
        start += count
    pieces = jnp.concatenate([own_w_ref[D:, :], other_w_ref[D:, :]], axis=1).astype(f32)
    proj = pieces[0:1] + pieces[1:2] + pieces[2:3]
    pre = jnp.dot(x_ref[...], u_ref[...], preferred_element_type=f32)
    sig = jax.nn.sigmoid(pre)
    hidden = (pre * sig).astype(bf16)
    keep_ref[:ROWS, : 2 * HID_DEV] = pre
    keep_ref[ROWS:, : 2 * HID_DEV] = jnp.broadcast_to(proj, (8, 2 * HID_DEV))
    value = jnp.sum(hidden.astype(f32) * proj, axis=1, keepdims=True)
    lane = iota((CAP, 128), 1)
    token = iota((CAP, TOK_DEV), 1).astype(f32)
    row = iota((16, TOK_DEV), 0)
    total = jnp.where((row == zh * 4 + y) & (grp == 0), base_ref[0:1, :], 0.0)
    for at, k, d in BLOCKS:
        note = keep_ref[at : at + CAP, 2 * HID_DEV :]
        gate = jnp.sum(jnp.where((lane >= 1 + 3 * zh) & (lane < 4 + 3 * zh), note, 0.0), axis=1, keepdims=True)
        term = gate * value[at : at + CAP]
        spread = jnp.sum(jnp.where(note[:, 0:1] == token, term, 0.0), axis=0, keepdims=True)
        total = total + jnp.where(row == (zh ^ k) * 4 + (y ^ d), spread, 0.0)
    part_ref[...] = total


def backward_kernel(info_ref, table_ref, x_ref, keep_ref, own_ref, send_ref, own_head_ref):
    zh, c, y = info_ref[1], info_ref[4], info_ref[3]
    table = table_ref[...]
    note = keep_ref[:ROWS, 2 * HID_DEV :]
    token = iota((CAP, TOK_DEV), 1).astype(f32)
    lane = iota((CAP, 128), 1)
    mine, gates = [], []
    for at, k, d in BLOCKS:
        block = ((zh ^ k) * 4 + (y ^ d)) * 2 + c
        values = table_ref[pl.ds(block, 1), :]
        part = keep_ref[at : at + CAP, 2 * HID_DEV :]
        mine.append(jnp.sum(jnp.where(part[:, 0:1] == token, values, 0.0), axis=1, keepdims=True))
        gates.append(
            jnp.sum(jnp.where((lane >= 1 + 3 * zh) & (lane < 4 + 3 * zh), part, 0.0), axis=1, keepdims=True)
        )
    mine = jnp.concatenate(mine, axis=0)
    gate = jnp.concatenate(gates, axis=0)
    hot = jnp.where(iota((ROWS, 32), 1).astype(f32) == note[:, 13:14], 1.0, 0.0).astype(bf16)
    found = jnp.zeros((ROWS, TOK_DEV), f32)
    for part in thirds(table):
        found = found + jnp.dot(hot, part.astype(bf16), preferred_element_type=f32)
    places = iota((ROWS, TOK_DEV), 1).astype(f32)
    theirs = jnp.sum(jnp.where(places == note[:, 14:15], found, 0.0), axis=1, keepdims=True)
    side = note[:, 15:16]
    margin = side * (mine - theirs)
    grad = -side * (64.0 * jax.nn.sigmoid(-margin)) * gate
    pre = keep_ref[:ROWS, : 2 * HID_DEV]
    proj = keep_ref[ROWS : ROWS + 1, : 2 * HID_DEV]
    sig = jax.nn.sigmoid(pre)
    hidden = (pre * sig).astype(bf16).astype(f32)
    hid_grad = jnp.sum(grad * hidden, axis=0, keepdims=True)
    pre_grad = (grad * proj * (sig * (1.0 + pre * (1.0 - sig)))).astype(bf16)
    out = lax.dot_general(x_ref[...], pre_grad, (((0,), (0,)), ((), ())), preferred_element_type=f32)
    own_ref[...] = out[:, :HID_DEV]
    send_ref[:D, :] = out[:, HID_DEV:]
    own_head_ref[...] = jnp.broadcast_to(hid_grad[:, :HID_DEV], (8, HID_DEV))
    send_ref[D:, :] = jnp.broadcast_to(hid_grad[:, HID_DEV:], (8, HID_DEV))


def loss_kernel(table_ref, pair_ref, out_ref):
    parts = jnp.concatenate([p.astype(bf16) for p in thirds(table_ref[...])], axis=0)

    def rewards_of(index):
        high = jnp.floor(index * (1.0 / TOK_DEV))
        low = index - high * TOK_DEV
        count = index.shape[1]
        row = iota((96, count), 0) & 31
        hot = jnp.where(row.astype(f32) == high, 1.0, 0.0).astype(bf16)
        found = lax.dot_general(parts, hot, (((0,), (0,)), ((), ())), preferred_element_type=f32)
        return jnp.sum(jnp.where(iota((TOK_DEV, count), 0).astype(f32) == low, found, 0.0), axis=0, keepdims=True)

    def step(r, total):
        def line(at):
            rows = [pair_ref[pl.ds(at + i, 1), :].astype(f32) for i in range(4)]
            return jnp.concatenate(rows, axis=1)

        margin = rewards_of(line(4 * r)) - rewards_of(line(4 * r + 32))
        return total + jnp.maximum(-margin, 0.0) + jnp.log1p(jnp.exp(-jnp.abs(margin)))

    total = lax.fori_loop(0, 8, step, jnp.zeros((1, 512), f32))
    out_ref[...] = jnp.broadcast_to(jnp.sum(total, axis=1, keepdims=True) * (1.0 / PAIRS), (1, 128))


def final_kernel(
    take_ref, up_ref, up_got_ref, down_ref, down_got_ref, own_ref, recv_ref, own_head_ref, head_ref, new_up_ref, new_down_ref
):
    step = own_ref[...] + recv_ref[:D, :]
    grad = own_head_ref[0:1] + recv_ref[D : D + 1, :]
    square = (HID_DEV, HID_DEV)
    column = jnp.sum(jnp.where(iota(square, 0) == iota(square, 1), grad, 0.0), axis=1, keepdims=True)
    head = head_ref[...].astype(f32)
    for wanted, ref in ((1, up_got_ref), (0, up_ref)):

        @pl.when(take_ref[0] == wanted)
        def _(ref=ref):
            new_up_ref[...] = (ref[...].astype(f32) + step).astype(bf16)

    for wanted, ref in ((1, down_got_ref), (0, down_ref)):

        @pl.when(take_ref[1] == wanted)
        def _(ref=ref):
            for j in range(D // HID_DEV):
                at = j * HID_DEV
                old = ref[at : at + HID_DEV, :].astype(f32)
                new_down_ref[:, at : at + HID_DEV] = (old + column * head[j : j + 1]).astype(bf16)


def pick_kernel(count, take_ref, *refs):
    got_refs, own_refs, out_refs = refs[:count], refs[count : 2 * count], refs[-count:]
    for i in range(count):

        @pl.when(take_ref[i] == 1)
        def _(i=i):
            out_refs[i][...] = got_refs[i][...]

        @pl.when(take_ref[i] == 0)
        def _(i=i):
            out_refs[i][...] = own_refs[i][...]


def split_kernel(take_ref, got_ref, own_ref, earlier_ref, up_ref, down_ref):
    for wanted, ref in ((1, got_ref), (0, own_ref)):

        @pl.when(take_ref[0] == wanted)
        def _(ref=ref):
            up_ref[...] = ref[:D, :]
            down_ref[...] = ref[D:, :]


def others_kernel(info_ref, rows_ref, *refs):
    zh = info_ref[1]
    for k in range(1, EXP_GRP):
        block = rows_ref[pl.ds(pl.multiple_of((zh ^ k) * CAP, CAP), CAP), :]
        refs[-1][CAP * (k - 1) : CAP * k, :] = block


def swap(block, axis, mask):
    count = lax.axis_size(axis)
    return lax.ppermute(block, axis, [(i, i ^ mask) for i in range(count)])


def picks(stages, got, own, *earlier, params=PARAMS):
    count = len(stages)
    return pl.pallas_call(
        functools.partial(pick_kernel, count),
        out_shape=[shape(o.shape, o.dtype) for o in own],
        in_specs=[SMEM] + [VMEM] * (2 * count) + [ANY] * len(earlier),
        out_specs=[VMEM] * count,
        compiler_params=params,
        cost_estimate=LIGHT,
        name="pick",
    )(jnp.concatenate([s[2] for s in stages]), *got, *own, *earlier)


def pick(stage, got, own, *earlier, params=PARAMS):
    return picks([stage], [got], [own], *earlier, params=params)[0]


def others(info, rows, *earlier):
    return pl.pallas_call(
        others_kernel,
        out_shape=shape((3 * CAP, WIDE), bf16),
        in_specs=[SMEM, VMEM] + [ANY] * len(earlier),
        out_specs=VMEM,
        compiler_params=PARAMS,
        cost_estimate=SPACED,
        name="others",
    )(info, rows, *earlier)


def body(tokens, routes, gate_values, old_group, move_mask, pair_index, reward_head, w_up, w_down, acc_up, acc_down):
    x, zl, zh, y, c = (lax.axis_index(a) for a in ("x", "zl", "zh", "y", "c"))
    info = jnp.stack([x * 4 + zl, zh, zh * 8 + y * 2 + c, y, c]).astype(jnp.int32)
    head = reward_head.reshape(D // 128, 128)
    pairs = pair_index.reshape(64, 128)
    mask = jnp.sum(jnp.where(jnp.arange(EXP_GRP) == zh, move_mask, 0))
    bit = [jnp.bitwise_and(jnp.right_shift(mask, i), 1) for i in range(4)]
    x1 = ("x", 1, jnp.bitwise_xor(bit[2], bit[3]).reshape(1))
    x3 = ("x", 3, bit[3].reshape(1))
    z1 = ("zl", 1, bit[0].reshape(1))
    z2 = ("zl", 2, bit[1].reshape(1))

    sent, own_rows, base, weights, accums = pl.pallas_call(
        dispatch_kernel,
        out_shape=[
            shape((EXP_GRP * CAP, WIDE), bf16),
            shape((CAP, WIDE), bf16),
            shape((8, TOK_DEV), f32),
            shape((D + 16, HID_DEV), bf16),
            shape((2 * D, HID_DEV), bf16),
        ],
        in_specs=[SMEM] * 3 + [VMEM] * 9,
        out_specs=[VMEM] * 5,
        compiler_params=pltpu.CompilerParams(vmem_limit_bytes=63 * 1024 * 1024),
        name="dispatch",
    )(
        old_group,
        move_mask,
        info,
        tokens,
        routes.T,
        gate_values.T,
        pairs,
        head,
        w_up[0],
        w_down[0],
        acc_up[0],
        acc_down[0],
    )
    arrived = lax.all_to_all(sent, "zh", 0, 0, tiled=True)
    got = swap(weights, *x1[:2])
    weights = pick(x1, got, weights)
    weights, own_rows, accums = lax.optimization_barrier((weights, own_rows, accums))
    got = swap(weights, *x3[:2])
    held = [own_rows] + [swap(own_rows, "y", d) for d in (1, 2, 3)]
    acc_got = swap(accums, *x1[:2])
    weights = pick(x3, got, weights)
    got = swap(weights, *z1[:2])
    accums = pick(x1, acc_got, accums, weights)
    acc_got = swap(accums, *x3[:2])
    weights = pick(z1, got, weights, accums, *held[1:])
    got = swap(weights, *z2[:2])
    rows = others(info, arrived, weights)
    held += [rows] + [swap(rows, "y", d) for d in (1, 2, 3)]
    weights = pick(z2, got, weights, rows)
    other_weights = swap(weights, "c", 1)
    up, down = pl.pallas_call(
        split_kernel,
        out_shape=[shape((D, HID_DEV), bf16)] * 2,
        in_specs=[SMEM, VMEM, VMEM, ANY],
        out_specs=[VMEM] * 2,
        compiler_params=PARAMS,
        cost_estimate=SPACED,
        name="pick_split",
    )(x3[2], acc_got, accums, weights)
    up_got = swap(up, *z1[:2])
    down_got = swap(down, *z2[:2])

    xs, keep, part = pl.pallas_call(
        forward_kernel,
        out_shape=[
            shape((ROWS, D), bf16),
            shape((ROWS + 8, 2 * HID_DEV + 128), f32),
            shape((16, TOK_DEV), f32),
        ],
        in_specs=[SMEM] + [VMEM] * 11,
        out_specs=[VMEM] * 3,
        scratch_shapes=[pltpu.VMEM((D, 2 * HID_DEV), bf16)],
        compiler_params=PARAMS,
        name="forward",
    )(info, base, weights, other_weights, *held)

    mine = lax.all_to_all(part, ("x", "y"), 0, 0, tiled=True)
    mine = jnp.broadcast_to(jnp.sum(mine, axis=0, keepdims=True), (16, TOK_DEV))
    mine = lax.all_to_all(mine, ("zl", "zh"), 0, 0, tiled=True)
    mine = jnp.broadcast_to(jnp.sum(mine, axis=0, keepdims=True), (32, TOK_DEV))
    up, down = picks([z1, z2], [up_got, down_got], [up, down], mine)
    mine, up, down = lax.optimization_barrier((mine, up, down))
    up_got = swap(up, *z2[:2])
    down_got = swap(down, *z1[:2])
    table = lax.all_to_all(mine, ("x", "y", "c"), 0, 0, tiled=True)

    own, send, own_head = pl.pallas_call(
        backward_kernel,
        out_shape=[shape((D, HID_DEV), f32), shape((D + 8, HID_DEV), f32), shape((8, HID_DEV), f32)],
        in_specs=[SMEM] + [VMEM] * 3,
        out_specs=[VMEM] * 3,
        compiler_params=WHOLE,
        cost_estimate=SPACED,
        name="backward",
    )(info, table, xs, keep)
    recv = swap(send, "c", 1)
    loss = pl.pallas_call(
        loss_kernel,
        out_shape=shape((1, 128), f32),
        in_specs=[VMEM] * 2,
        out_specs=VMEM,
        compiler_params=PARAMS,
        cost_estimate=SPACED,
        name="loss",
    )(table, pairs)
    new_up, new_down = pl.pallas_call(
        final_kernel,
        out_shape=[shape((D, HID_DEV), bf16), shape((HID_DEV, D), bf16)],
        in_specs=[SMEM] + [VMEM] * 8,
        out_specs=[VMEM] * 2,
        compiler_params=PARAMS,
        name="final",
    )(jnp.concatenate([z2[2], z1[2]]), up, up_got, down, down_got, own, recv, own_head, head)
    return new_up[None], new_down[None], loss[0, 0]


def solution(mesh):
    fine = Mesh(mesh.devices.reshape(4, 4, 4, 4, 2), ("x", "zl", "zh", "y", "c"))
    grp, ep = ("x", "zl"), ("zh", "y", "c")
    return jax.shard_map(
        body,
        mesh=fine,
        in_specs=(P(ep, None), P(ep, None), P(ep, None), P(), P(), P(), P())
        + (P(grp, None, ep), P(grp, ep, None)) * 2,
        out_specs=(P(grp, None, ep), P(grp, ep, None), P()),
        check_vma=False,
    )
```
